32 devices in a mesh: tm: 32 (over z, y, x, core), space: 1.
Axes of the slice: x: 2, y: 2, z: 4, core: 2. Of those that a mesh axis runs over, the one named last changes fastest.
Arguments:
- fields: bfloat16 [1024, 8, 8, 256], P('tm', None, 'space'), may hold values from -6 to 6
- conv_in: bfloat16 [64, 8, 3, 3], replicated, may hold values from -0.75 to 0.75
- conv_mid: bfloat16 [128, 64, 3, 3], replicated, may hold values from -0.25 to 0.25
- obs_gain: bfloat16 [2, 64, 128, 256], P('space'), may hold values from -0.0029296875 to 0.0029296875
- transition: float32 [256, 256], replicated, as said below
- back_gain: float32 [256, 256], replicated, as said below
- retain: float32 [1024, 256], P('tm'), may hold values from 0.5 to 1.03
Outputs:
- filtered: float32 [1024, 256], P(('tm', 'space'))
- smoothed: float32 [1024, 256], P(('tm', 'space'))
The draws below stay inside these ranges and needn't reach their ends.
Inputs may be any that keep to these rules, and one draw needn't show every extreme that they name: The spectral norm of transition is below one. The spectral norm of back_gain is below one.
All inputs are finite; a program needn't handle non-finite values.
Results may differ from the reference program's by a relative error of at most 0.0045.
Values may be sent and summed in bfloat16 or wider, within the bound.
A program may use at most 192 MiB of HBM per device.

```python
import jax
import jax.numpy as jnp
from jax import lax

CH_IN = 8
C1 = 64
C2 = 128
PATTERN_COUNT = 256
HOUR_DEV = 32
LON = 256
CLOCK_SPAN = 1024
LAT = 8
LAT4 = 2
LON4 = 64
N_TM = 32


def decay_rates(key):
    key_slow, key_long, key_fast = jax.random.split(key, 3)
    share = 0.5
    is_slow = jax.random.bernoulli(key_slow, share, (PATTERN_COUNT // 2,))
    log_span = jax.random.uniform(key_long, (PATTERN_COUNT // 2,), jnp.float32, jnp.log(0.2), jnp.log(1.5))
    slow_rate = jnp.exp(-jnp.exp(log_span) / CLOCK_SPAN)
    fast_span = jax.random.uniform(key_fast, (PATTERN_COUNT // 2,), jnp.float32, 25.0, 50.0)
    fast_rate = jnp.exp(-1.0 / fast_span)
    return jnp.where(is_slow, slow_rate, fast_rate)


def rotation_mix(key, rates):
    key_turn, key_sign, key_mirror = jax.random.split(key, 3)
    magnitude = jax.random.uniform(key_turn, (PATTERN_COUNT // 2,), jnp.float32, 0.25, 1.0)
    flipped = jnp.where(jax.random.bernoulli(key_sign, 0.5, (PATTERN_COUNT // 2,)), 1.0, -1.0)
    angles = magnitude * flipped
    indices = jnp.arange(PATTERN_COUNT)
    pair_of = indices // 2
    parity = indices % 2
    same_pair = pair_of[:, None] == pair_of[None, :]
    radius = rates[pair_of][:, None]
    cosine = jnp.cos(angles)[pair_of][:, None]
    sine_part = jnp.sin(angles)[pair_of][:, None]
    on_diag = parity[:, None] == parity[None, :]
    off_part = jnp.where(parity[:, None] == 1, sine_part, -sine_part)
    rotated = jnp.where(same_pair, radius * jnp.where(on_diag, cosine, off_part), 0.0)
    mirror = jax.random.normal(key_mirror, (PATTERN_COUNT,), jnp.float32)
    length = jnp.sum(mirror * mirror)
    right_prod = jnp.sum(rotated * mirror[None, :], axis=1)
    left_prod = jnp.sum(mirror[:, None] * rotated, axis=0)
    middle = jnp.sum(mirror * right_prod)
    mixed = rotated - 2.0 / length * mirror[:, None] * left_prod[None, :]
    mixed = mixed - 2.0 / length * right_prod[:, None] * mirror[None, :]
    return mixed + 4.0 / (length * length) * middle * mirror[:, None] * mirror[None, :]


def draw_transition(key, part):
    return rotation_mix(jax.random.fold_in(key, 11), decay_rates(jax.random.fold_in(key, 12)))


def draw_back_gain(key, part):
    return rotation_mix(jax.random.fold_in(key, 21), decay_rates(jax.random.fold_in(key, 22)))


def draw_retain(key, part):
    storm_seed, amount_seed, level_seed = jax.random.split(jax.random.fold_in(key, 31), 3)
    storm_chance = 4.0 / CLOCK_SPAN
    storm_events = jax.random.uniform(storm_seed, (CLOCK_SPAN, PATTERN_COUNT), jnp.float32) < storm_chance
    water_amount = jax.random.uniform(amount_seed, (CLOCK_SPAN, PATTERN_COUNT), jnp.float32, 0.5, 0.8)
    drizzle_level = jax.random.uniform(level_seed, (CLOCK_SPAN, PATTERN_COUNT), jnp.float32, 0.97, 1.03)
    return jnp.where(storm_events, water_amount, drizzle_level)


def levels(key, dims, cuts, least, top_value):
    def one(dim, shards_of):
        heights = jax.random.uniform(jax.random.fold_in(jax.random.fold_in(key, 6), dim), (shards_of,), jnp.float32, least / len(cuts), top_value / len(cuts))
        return jnp.repeat(jnp.exp(heights), dims[dim] // shards_of).reshape((-1,) + (1,) * (len(dims) - dim - 1))

    loudness = one(*cuts[0])
    for cut in cuts[1:]:
        loudness = loudness * one(*cut)
    return loudness


def normal_values(rng, extent, scale, reach, pieces=(), held_as=jnp.bfloat16):
    values = jax.random.normal(rng, extent, jnp.float32) * scale
    if len(pieces) > 0:
        values = levels(rng, extent, pieces, -0.22, 0.18) * values
    return jnp.clip(values, min=-reach, max=reach).astype(held_as)


def setup_inputs(seed: int = 0) -> dict:
    streams_of = jax.random.split(jax.random.key(seed), 8)
    fields = normal_values(streams_of[0], (CLOCK_SPAN, CH_IN, LAT, LON), 1.0, 6.0, ((0, 32),))
    conv_in = normal_values(streams_of[1], (C1, CH_IN, 3, 3), (CH_IN * 9) ** -0.5, 0.75)
    conv_mid = normal_values(streams_of[2], (C2, C1, 3, 3), (C1 * 9) ** -0.5, 0.25)
    obs_gain = normal_values(streams_of[3], (LAT4, LON4, C2, PATTERN_COUNT), (LAT4 * LON4 * C2 * 256) ** -0.5, 0.0029296875)
    transition = draw_transition(jax.random.fold_in(streams_of[7], 71), 0)
    back_gain = draw_back_gain(jax.random.fold_in(streams_of[7], 71), 0)
    retain = draw_retain(jax.random.fold_in(streams_of[7], 71), 0)
    return {"fields": fields, "conv_in": conv_in, "conv_mid": conv_mid, "obs_gain": obs_gain, "transition": transition, "back_gain": back_gain, "retain": retain}


precise = lax.Precision.HIGHEST


def encode_block(block, conv_in, conv_mid, obs_gain):
    hidden = lax.conv_general_dilated(block, conv_in, (2, 2), ((1, 1), (1, 1)), dimension_numbers=("NCHW", "OIHW", "NCHW"), preferred_element_type=jnp.float32)
    hidden = jax.nn.silu(hidden).astype(jnp.bfloat16)
    encoded = lax.conv_general_dilated(hidden, conv_mid, (2, 2), ((1, 1), (1, 1)), dimension_numbers=("NCHW", "OIHW", "NHWC"), preferred_element_type=jnp.float32)
    encoded = jax.nn.silu(encoded).astype(jnp.bfloat16)
    return jnp.einsum("shwc,hwcm->sm", encoded.astype(jnp.float32), obs_gain.astype(jnp.float32))


def reference(fields, conv_in, conv_mid, obs_gain, transition, back_gain, retain):
    blocks = fields.reshape((N_TM, HOUR_DEV, CH_IN, LAT, LON))
    increments = lax.map(lambda block: encode_block(block, conv_in, conv_mid, obs_gain), blocks)
    increments = increments.reshape((CLOCK_SPAN, PATTERN_COUNT))

    def forward_step(state, inputs):
        gate_row, increment = inputs
        state = gate_row * jnp.dot(transition, state, precision=precise) + increment
        return state, state

    final_state, filtered = lax.scan(forward_step, jnp.zeros((PATTERN_COUNT,), jnp.float32), (retain, increments))
    joined = jnp.dot(back_gain, transition, precision=precise)
    sources = filtered - jnp.dot(filtered, joined.T, precision=precise)
    boundary = jnp.dot(transition, final_state, precision=precise)

    def back_step(state, source):
        state = source + jnp.dot(back_gain, state, precision=precise)
        return state, state

    first_state, smoothed = lax.scan(back_step, boundary, sources, reverse=True)
    return filtered, smoothed
```

```python
import functools

import jax
import jax.numpy as jnp
from jax import lax
from jax.experimental import pallas as pl
from jax.experimental.pallas import tpu as pltpu
from jax.sharding import PartitionSpec as P

precise = lax.Precision.HIGHEST
F32 = jnp.float32
BF16 = jnp.bfloat16
SEGMENTS = 4
ROWS = 8


def shifted(value, axis, steps):
    count = lax.axis_size(axis)
    leading, last = (max(0, -steps), min(count, count - steps))
    return lax.ppermute(value, axis, [(source, source + steps) for source in range(leading, last)])


def conv_stride(images, kernel, layout_out):
    return lax.conv_general_dilated(
        images,
        kernel,
        (2, 2),
        ((0, 0), (1, 1)),
        dimension_numbers=("NCHW", "OIHW", layout_out),
        preferred_element_type=jnp.float32,
    )


def split_wide(matrix):
    high = matrix.astype(BF16)
    low = (matrix - high.astype(F32)).astype(BF16)
    return jnp.concatenate([high, low], axis=1)


def times(rows, wide):
    count = rows.shape[0]
    size = wide.shape[1] // 2
    high = rows.astype(BF16).astype(F32)
    parts = jnp.concatenate([high, rows - high], axis=0).astype(BF16)
    full = jnp.dot(parts, wide, preferred_element_type=F32)
    return full[:count, :size] + full[count:, :size] + full[:count, size:]


def local_kernel(transition_ref, gain_ref, retain_ref, seg_ref, total_ref, power_ref, chain):
    hours, size = retain_ref.shape
    span = hours // SEGMENTS
    moved = transition_ref[...].T
    wide = split_wide(moved)
    for k in range(SEGMENTS):
        chain[k] = moved * retain_ref[pl.ds(k * span, 1), :]

    def one(step, carry):
        for k in range(SEGMENTS):
            chain[k] = times(chain[k], wide) * retain_ref[pl.ds(k * span + step, 1), :]
        return carry

    lax.fori_loop(1, span, one, 0)
    for k in range(1, SEGMENTS):
        seg_ref[k - 1] = split_wide(chain[k])
    prefix = chain[0]
    for k in range(1, SEGMENTS):
        seg_ref[SEGMENTS - 2 + k] = split_wide(prefix)
        prefix = times(prefix, seg_ref[k - 1])
    total_ref[...] = prefix
    power = gain_ref[...].T
    for k in range(power_ref.shape[0]):
        power_wide = split_wide(power)
        power_ref[k] = power_wide
        if k < power_ref.shape[0] - 1:
            power = times(power, power_wide)


def local_matrices(transition, back_gain, retain, powers):
    size = transition.shape[0]
    return pl.pallas_call(
        local_kernel,
        out_shape=(
            jax.ShapeDtypeStruct((2 * SEGMENTS - 2, size, 2 * size), BF16),
            jax.ShapeDtypeStruct((size, size), F32),
            jax.ShapeDtypeStruct((powers, size, 2 * size), BF16),
        ),
        in_specs=[pl.BlockSpec(memory_space=pltpu.VMEM)] * 3,
        out_specs=[pl.BlockSpec(memory_space=pltpu.VMEM)] * 3,
        scratch_shapes=[pltpu.VMEM((SEGMENTS, size, size), F32)],
        compiler_params=pltpu.CompilerParams(vmem_limit_bytes=32 * 1024 * 1024),
    )(transition, back_gain, retain)


def widened(row):
    return jnp.broadcast_to(row, (ROWS, row.shape[1]))


def solve_back(rows, power_ref, first, steps):
    for k in range(steps):
        stride = 1 << k
        filler = jnp.zeros((stride, rows.shape[1]), F32)
        ahead = jnp.concatenate([rows[stride:], filler], axis=0)
        rows = rows + times(ahead, power_ref[first + k])
    return rows


def chain_kernel(
    count,
    levels,
    hour_levels,
    inc_ref,
    retain_ref,
    transition_ref,
    seg_ref,
    jump_ref,
    power_ref,
    filtered_ref,
    smoothed_ref,
    out_box,
    in_box,
    back_out,
    back_box,
    send_sems,
    recv_sems,
    back_send,
    back_recv,
):
    hours, size = inc_ref.shape
    span = hours // SEGMENTS
    place = lax.axis_index("tm")

    barrier = pltpu.get_barrier_semaphore()

    def greet(step, carry):
        peer = lax.rem(place + step, count)
        pl.semaphore_signal(
            barrier, inc=1, device_id={"tm": peer}, device_id_type=pl.DeviceIdType.MESH
        )
        return carry

    lax.fori_loop(1, count, greet, 0)

    wide = split_wide(transition_ref[...].T)
    increments = inc_ref[...]
    gates = retain_ref[...]
    blank = jnp.zeros((ROWS - SEGMENTS, size), F32)

    def of_step(rows, step):
        picked = [rows[k * span + step : k * span + step + 1] for k in range(SEGMENTS)]
        return jnp.concatenate(picked + [blank], axis=0)

    gate_rows = [of_step(gates, step) for step in range(span)]
    inc_rows = [of_step(increments, step) for step in range(span)]
    state = inc_rows[0]
    for step in range(1, span):
        state = times(state, wide) * gate_rows[step] + inc_rows[step]
    starts = [jnp.zeros((1, size), F32)]
    carry = state[0:1]
    for k in range(1, SEGMENTS):
        starts.append(carry)
        carry = times(widened(carry), seg_ref[k - 1])[0:1] + state[k : k + 1]

    pl.semaphore_wait(barrier, count - 1)

    def push(slot, distance, row):
        out_box[slot] = row
        copy = pltpu.make_async_remote_copy(
            src_ref=out_box.at[slot],
            dst_ref=in_box.at[slot],
            send_sem=send_sems.at[slot],
            recv_sem=recv_sems.at[slot],
            device_id={"tm": lax.rem(place + distance, count)},
            device_id_type=pl.DeviceIdType.MESH,
        )
        copy.start()
        return copy

    copies = [push(0, 1, carry), push(1, 2, carry)]
    entering = jnp.zeros((1, size), F32)
    for level in range(levels):
        jump = split_wide(jump_ref[level])
        if level == 0:
            copies[0].wait_recv()
            entering = jnp.where(place >= 1, in_box[0], 0.0)
        else:
            copies.append(push(level + 1, 1 << level, entering))
        copies[level + 1].wait_recv()
        far = jnp.where(place >= (2 if level == 0 else 1 << level), in_box[level + 1], 0.0)
        entering = entering + times(widened(far), jump)[0:1]

    opened = [entering]
    for k in range(1, SEGMENTS):
        opened.append(
            times(widened(entering), seg_ref[SEGMENTS - 2 + k])[0:1] + starts[k]
        )
    state = jnp.concatenate(opened + [blank], axis=0)
    states = []
    for step in range(span):
        state = times(state, wide) * gate_rows[step] + inc_rows[step]
        states.append(state)
    filtered = jnp.concatenate(
        [states[step][k : k + 1] for k in range(SEGMENTS) for step in range(span)], axis=0
    )
    filtered_ref[...] = filtered
    gain = power_ref[0]
    carried = times(filtered, wide)
    sources = filtered - times(carried, gain)
    final = place == count - 1
    last_row = carried[hours - 1 : hours]
    boundary = jnp.where(final, last_row, jnp.zeros_like(last_row))
    mask = lax.broadcasted_iota(jnp.int32, (hours, 1), 0) == hours - 1

    def with_end(row):
        return sources + jnp.where(mask, times(widened(row), gain)[0:1], 0.0)

    first_pass = solve_back(with_end(boundary), power_ref, 0, hour_levels)
    back_out[0] = first_pass[0:1]

    def back_copy(step):
        return pltpu.make_async_remote_copy(
            src_ref=back_out.at[0],
            dst_ref=back_box.at[step],
            send_sem=back_send.at[step],
            recv_sem=back_recv.at[step],
            device_id={"tm": lax.rem(place + count - 1 - step, count)},
            device_id_type=pl.DeviceIdType.MESH,
        )

    def back_start(step, carry):
        back_copy(step).start()
        return carry

    def back_wait(step, carry):
        back_copy(step).wait()
        return carry

    lax.fori_loop(0, count - 1, back_start, 0)
    lax.fori_loop(0, count - 1, back_wait, 0)
    rows = jnp.concatenate(
        [back_box[step] for step in range(count - 1)] + [jnp.zeros((1, size), F32)], axis=0
    )
    later = lax.broadcasted_iota(jnp.int32, (count, 1), 0) < count - 1 - place
    rows = jnp.where(later, rows, 0.0)
    after = solve_back(rows, power_ref, hour_levels, levels)[0:1]
    smoothed_ref[...] = solve_back(with_end(after + boundary), power_ref, 0, hour_levels)
    for copy in copies:
        copy.wait_send()


def chains(increments, retain, transition, segs, jumps, powers, levels, hour_levels):
    count = lax.axis_size("tm")
    hours, size = increments.shape
    return pl.pallas_call(
        functools.partial(chain_kernel, count, levels, hour_levels),
        out_shape=(
            jax.ShapeDtypeStruct((hours, size), F32),
            jax.ShapeDtypeStruct((hours, size), F32),
        ),
        in_specs=[pl.BlockSpec(memory_space=pltpu.VMEM)] * 6,
        out_specs=[pl.BlockSpec(memory_space=pltpu.VMEM)] * 2,
        scratch_shapes=[
            pltpu.VMEM((levels + 1, 1, size), F32),
            pltpu.VMEM((levels + 1, 1, size), F32),
            pltpu.VMEM((1, 1, size), F32),
            pltpu.VMEM((count, 1, size), F32),
            pltpu.SemaphoreType.DMA((levels + 1,)),
            pltpu.SemaphoreType.DMA((levels + 1,)),
            pltpu.SemaphoreType.DMA((count,)),
            pltpu.SemaphoreType.DMA((count,)),
        ],
        compiler_params=pltpu.CompilerParams(
            collective_id=0, has_side_effects=True, vmem_limit_bytes=32 * 1024 * 1024
        ),
    )(increments, retain, transition, segs, jumps, powers)


def per_device(fields, conv_in, conv_mid, obs_gain, transition, back_gain, retain):
    hour_count = fields.shape[0]
    count = lax.axis_size("tm")
    levels = (count - 1).bit_length()
    hour_levels = (hour_count - 1).bit_length()
    segs, total, powers = local_matrices(transition, back_gain, retain, levels + hour_levels)
    jump = shifted(total, "tm", 1)
    jumps = [jump]
    older = shifted(total, "tm", 2)
    for level in range(1, levels):
        jump = jnp.dot(older, jump, precision=precise)
        jumps.append(jump)
        if level < levels - 1:
            older = shifted(jump, "tm", 1 << level)

    if lax.axis_size("space") == 1:
        below_rows = jnp.zeros_like(fields[:, :, -3:, :])
    else:
        below_rows = shifted(fields[:, :, -3:, :], "space", 1)
    hidden = conv_stride(
        jnp.concatenate([below_rows[:, :, -1:, :], fields], axis=2), conv_in, "NCHW"
    )
    hidden = jax.nn.silu(hidden).astype(jnp.bfloat16)
    below_hidden = jax.nn.silu(conv_stride(below_rows, conv_in, "NCHW")).astype(jnp.bfloat16)
    encoded = conv_stride(jnp.concatenate([below_hidden, hidden], axis=2), conv_mid, "NHWC")
    encoded = jax.nn.silu(encoded).astype(jnp.bfloat16)
    share = hour_count // lax.axis_size("space")
    partial_sum = jnp.einsum("shwc,hwcm->sm", encoded, obs_gain, preferred_element_type=jnp.float32)
    increments = lax.psum(partial_sum, "space")
    filtered, smoothed = chains(
        increments, retain, transition, segs, jnp.stack(jumps), powers, levels, hour_levels
    )
    offset = lax.axis_index("space") * share
    filtered = lax.dynamic_slice_in_dim(filtered, offset, share, 0)
    smoothed = lax.dynamic_slice_in_dim(smoothed, offset, share, 0)
    return (filtered, smoothed)


def solution(mesh):
    placed = (
        P("tm", None, "space", None),
        P(),
        P(),
        P("space", None, None, None),
        P(),
        P(),
        P("tm", None),
    )
    return jax.shard_map(
        per_device,
        mesh=mesh,
        in_specs=placed,
        out_specs=(P(("tm", "space"), None), P(("tm", "space"), None)),
        check_vma=False,
    )
```

```python
import functools

import jax
import jax.numpy as jnp
from jax import lax
from jax.experimental import pallas as pl
from jax.experimental.pallas import tpu as pltpu
from jax.sharding import PartitionSpec as P

precise = lax.Precision.HIGHEST
F32 = jnp.float32
BF16 = jnp.bfloat16
SEGMENTS = 4
ROWS = 8


def shifted(value, axis, steps):
    count = lax.axis_size(axis)
    leading, last = (max(0, -steps), min(count, count - steps))
    return lax.ppermute(value, axis, [(source, source + steps) for source in range(leading, last)])


def conv_stride(images, kernel, layout_out):
    return lax.conv_general_dilated(
        images,
        kernel,
        (2, 2),
        ((0, 0), (1, 1)),
        dimension_numbers=("NCHW", "OIHW", layout_out),
        preferred_element_type=jnp.float32,
    )


def split_wide(matrix):
    high = matrix.astype(BF16)
    low = (matrix - high.astype(F32)).astype(BF16)
    return jnp.concatenate([high, low], axis=1)


def times(rows, wide):
    count = rows.shape[0]
    size = wide.shape[1] // 2
    high = rows.astype(BF16).astype(F32)
    parts = jnp.concatenate([high, rows - high], axis=0).astype(BF16)
    full = jnp.dot(parts, wide, preferred_element_type=F32)
    return full[:count, :size] + full[count:, :size] + full[:count, size:]


def local_kernel(transition_ref, gain_ref, retain_ref, seg_ref, total_ref, power_ref, chain):
    hours, size = retain_ref.shape
    span = hours // SEGMENTS
    moved = transition_ref[...].T
    wide = split_wide(moved)
    for k in range(SEGMENTS):
        chain[k] = moved * retain_ref[pl.ds(k * span, 1), :]

    def one(step, carry):
        for k in range(SEGMENTS):
            chain[k] = times(chain[k], wide) * retain_ref[pl.ds(k * span + step, 1), :]
        return carry

    lax.fori_loop(1, span, one, 0)
    for k in range(1, SEGMENTS):
        seg_ref[k - 1] = split_wide(chain[k])
    prefix = chain[0]
    for k in range(1, SEGMENTS):
        seg_ref[SEGMENTS - 2 + k] = split_wide(prefix)
        prefix = times(prefix, seg_ref[k - 1])
    total_ref[...] = prefix
    power = gain_ref[...].T
    for k in range(power_ref.shape[0]):
        power_wide = split_wide(power)
        power_ref[k] = power_wide
        if k < power_ref.shape[0] - 1:
            power = times(power, power_wide)


def local_matrices(transition, back_gain, retain, powers):
    size = transition.shape[0]
    return pl.pallas_call(
        local_kernel,
        out_shape=(
            jax.ShapeDtypeStruct((2 * SEGMENTS - 2, size, 2 * size), BF16),
            jax.ShapeDtypeStruct((size, size), F32),
            jax.ShapeDtypeStruct((powers, size, 2 * size), BF16),
        ),
        in_specs=[pl.BlockSpec(memory_space=pltpu.VMEM)] * 3,
        out_specs=[pl.BlockSpec(memory_space=pltpu.VMEM)] * 3,
        scratch_shapes=[pltpu.VMEM((SEGMENTS, size, size), F32)],
        compiler_params=pltpu.CompilerParams(vmem_limit_bytes=32 * 1024 * 1024),
    )(transition, back_gain, retain)


def widened(row):
    return jnp.broadcast_to(row, (ROWS, row.shape[1]))


def solve_back(rows, power_ref, first, steps):
    for k in range(steps):
        stride = 1 << k
        filler = jnp.zeros((stride, rows.shape[1]), F32)
        ahead = jnp.concatenate([rows[stride:], filler], axis=0)
        rows = rows + times(ahead, power_ref[first + k])
    return rows


def chain_kernel(
    count,
    levels,
    hour_levels,
    inc_ref,
    retain_ref,
    transition_ref,
    seg_ref,
    jump_ref,
    power_ref,
    filtered_ref,
    smoothed_ref,
    out_box,
    in_box,
    back_out,
    back_box,
    send_sems,
    recv_sems,
    back_send,
    back_recv,
):
    hours, size = inc_ref.shape
    span = hours // SEGMENTS
    place = lax.axis_index("tm")

    barrier = pltpu.get_barrier_semaphore()

    def greet(step, carry):
        peer = lax.rem(place + step, count)
        pl.semaphore_signal(
            barrier, inc=1, device_id={"tm": peer}, device_id_type=pl.DeviceIdType.MESH
        )
        return carry

    lax.fori_loop(1, count, greet, 0)

    wide = split_wide(transition_ref[...].T)
    increments = inc_ref[...]
    gates = retain_ref[...]
    blank = jnp.zeros((ROWS - SEGMENTS, size), F32)

    def of_step(rows, step):
        picked = [rows[k * span + step : k * span + step + 1] for k in range(SEGMENTS)]
        return jnp.concatenate(picked + [blank], axis=0)

    gate_rows = [of_step(gates, step) for step in range(span)]
    inc_rows = [of_step(increments, step) for step in range(span)]
    state = inc_rows[0]
    for step in range(1, span):
        state = times(state, wide) * gate_rows[step] + inc_rows[step]
    starts = [jnp.zeros((1, size), F32)]
    carry = state[0:1]
    for k in range(1, SEGMENTS):
        starts.append(carry)
        carry = times(widened(carry), seg_ref[k - 1])[0:1] + state[k : k + 1]

    pl.semaphore_wait(barrier, count - 1)

    def push(slot, distance, row):
        out_box[slot] = row
        copy = pltpu.make_async_remote_copy(
            src_ref=out_box.at[slot],
            dst_ref=in_box.at[slot],
            send_sem=send_sems.at[slot],
            recv_sem=recv_sems.at[slot],
            device_id={"tm": lax.rem(place + distance, count)},
            device_id_type=pl.DeviceIdType.MESH,
        )
        copy.start()
        return copy

    copies = [push(0, 1, carry), push(1, 2, carry)]
    entering = jnp.zeros((1, size), F32)
    for level in range(levels):
        jump = split_wide(jump_ref[level])
        if level == 0:
            copies[0].wait_recv()
            entering = jnp.where(place >= 1, in_box[0], 0.0)
        else:
            copies.append(push(level + 1, 1 << level, entering))
        copies[level + 1].wait_recv()
        far = jnp.where(place >= (2 if level == 0 else 1 << level), in_box[level + 1], 0.0)
        entering = entering + times(widened(far), jump)[0:1]

    opened = [entering]
    for k in range(1, SEGMENTS):
        opened.append(
            times(widened(entering), seg_ref[SEGMENTS - 2 + k])[0:1] + starts[k]
        )
    state = jnp.concatenate(opened + [blank], axis=0)
    states = []
    for step in range(span):
        state = times(state, wide) * gate_rows[step] + inc_rows[step]
        states.append(state)
    filtered = jnp.concatenate(
        [states[step][k : k + 1] for k in range(SEGMENTS) for step in range(span)], axis=0
    )
    filtered_ref[...] = filtered
    gain = power_ref[0]
    carried = times(filtered, wide)
    sources = filtered - times(carried, gain)
    final = place == count - 1
    last_row = carried[hours - 1 : hours]
    boundary = jnp.where(final, last_row, jnp.zeros_like(last_row))
    mask = lax.broadcasted_iota(jnp.int32, (hours, 1), 0) == hours - 1

    def with_end(row):
        return sources + jnp.where(mask, times(widened(row), gain)[0:1], 0.0)

    first_pass = solve_back(with_end(boundary), power_ref, 0, hour_levels)
    back_out[0] = first_pass[0:1]

    def back_copy(step):
        return pltpu.make_async_remote_copy(
            src_ref=back_out.at[0],
            dst_ref=back_box.at[step],
            send_sem=back_send.at[step],
            recv_sem=back_recv.at[step],
            device_id={"tm": lax.rem(place + count - 1 - step, count)},
            device_id_type=pl.DeviceIdType.MESH,
        )

    def back_start(step, carry):
        back_copy(step).start()
        return carry

    def back_wait(step, carry):
        back_copy(step).wait()
        return carry

    lax.fori_loop(0, count - 1, back_start, 0)
    lax.fori_loop(0, count - 1, back_wait, 0)
    rows = jnp.concatenate(
        [back_box[step] for step in range(count - 1)] + [jnp.zeros((1, size), F32)], axis=0
    )
    later = lax.broadcasted_iota(jnp.int32, (count, 1), 0) < count - 1 - place
    rows = jnp.where(later, rows, 0.0)
    after = solve_back(rows, power_ref, hour_levels, levels)[0:1]
    smoothed_ref[...] = solve_back(with_end(after + boundary), power_ref, 0, hour_levels)
    for copy in copies:
        copy.wait_send()


def chains(increments, retain, transition, segs, jumps, powers, levels, hour_levels):
    count = lax.axis_size("tm")
    hours, size = increments.shape
    return pl.pallas_call(
        functools.partial(chain_kernel, count, levels, hour_levels),
        out_shape=(
            jax.ShapeDtypeStruct((hours, size), F32),
            jax.ShapeDtypeStruct((hours, size), F32),
        ),
        in_specs=[pl.BlockSpec(memory_space=pltpu.VMEM)] * 6,
        out_specs=[pl.BlockSpec(memory_space=pltpu.VMEM)] * 2,
        scratch_shapes=[
            pltpu.VMEM((levels + 1, 1, size), F32),
            pltpu.VMEM((levels + 1, 1, size), F32),
            pltpu.VMEM((1, 1, size), F32),
            pltpu.VMEM((count, 1, size), F32),
            pltpu.SemaphoreType.DMA((levels + 1,)),
            pltpu.SemaphoreType.DMA((levels + 1,)),
            pltpu.SemaphoreType.DMA((count,)),
            pltpu.SemaphoreType.DMA((count,)),
        ],
        compiler_params=pltpu.CompilerParams(
            collective_id=0, has_side_effects=True, vmem_limit_bytes=32 * 1024 * 1024
        ),
    )(increments, retain, transition, segs, jumps, powers)


GROUP = 4


def silu(value):
    half = 0.5 * value
    return half + half * jnp.tanh(half)


def one_hot(hits):
    return jnp.where(hits, 1.0, 0.0).astype(BF16)


def fill_weights(conv_in_ref, conv_mid_ref, picks_ref, first_ref, second_ref):
    half, columns = picks_ref.shape[0] // 3, picks_ref.shape[1]
    place = lax.broadcasted_iota(jnp.int32, (half, columns), 0)
    column = lax.broadcasted_iota(jnp.int32, (half, columns), 1)
    j = jnp.where(place < half // 2, 2 * place, 2 * place - half + 1)
    for dx in range(3):
        picks_ref[dx * half : (dx + 1) * half, :] = one_hot(column == 2 * j + dx - 1)
    channels, outs = conv_in_ref.shape[2:]
    depth = first_ref.shape[1] // (2 * GROUP - 1)
    rows = depth // channels
    source = lax.broadcasted_iota(jnp.int32, (depth, 3 * channels), 0)
    tap = lax.broadcasted_iota(jnp.int32, (depth, 3 * channels), 1)
    same = (source // rows) == (tap % channels)
    margin = (GROUP - 1) * depth
    first_ref[...] = jnp.zeros(first_ref.shape, BF16)
    for dx in range(3):
        taps = jnp.concatenate([conv_in_ref[dy, dx].astype(F32) for dy in range(3)], axis=0)
        for r in range(rows // 2):
            spread = one_hot(same & (source % rows == 2 * r + tap // channels - 1))
            block = jnp.dot(spread, taps.astype(BF16), preferred_element_type=F32)
            first_ref[dx, margin : margin + depth, r * outs : (r + 1) * outs] = block.astype(BF16)
    inner, outs = conv_mid_ref.shape[2:]
    second_ref[...] = jnp.zeros(second_ref.shape, BF16)
    for dx in range(3):
        for out_row in range(rows // 4):
            for dy in range(3):
                r = 2 * out_row + dy - 1
                if 0 <= r < rows // 2:
                    second_ref[
                        dx, r * inner : (r + 1) * inner, out_row * outs : (out_row + 1) * outs
                    ] = conv_mid_ref[dy, dx]


def encode_kernel(
    field_ref,
    conv_in_ref,
    conv_mid_ref,
    gain_hbm,
    out_ref,
    gain_ref,
    encoded_ref,
    picks_ref,
    first_ref,
    second_ref,
    gain_sem,
):
    hours = out_ref.shape[0]
    depth = field_ref.shape[0] // hours
    half = picks_ref.shape[0] // 3
    quarter = half // 2
    copy = pltpu.make_async_copy(gain_hbm, gain_ref, gain_sem)
    copy.start()
    fill_weights(conv_in_ref, conv_mid_ref, picks_ref, first_ref, second_ref)

    def group(index, carry):
        images = field_ref[pl.ds(pl.multiple_of(index * GROUP * depth, GROUP * depth), GROUP * depth), :]
        picked = lax.dot_general(
            picks_ref[...], images, (((1,), (1,)), ((), ())), preferred_element_type=F32
        ).astype(BF16)
        taps = ([], [], [])
        for hour in range(GROUP):
            low = (GROUP - 1 - hour) * depth
            total = None
            for dx in range(3):
                part = jnp.dot(
                    picked[dx * half : (dx + 1) * half],
                    first_ref[dx, low : low + GROUP * depth, :],
                    preferred_element_type=F32,
                )
                total = part if total is None else total + part
            hidden = silu(total)
            odd = hidden[quarter:]
            before = jnp.concatenate(
                [jnp.zeros((1, hidden.shape[1]), F32), odd[: quarter - 1]], axis=0
            )
            taps[0].append(before.astype(BF16))
            taps[1].append(hidden[:quarter].astype(BF16))
            taps[2].append(odd.astype(BF16))
        total = None
        for dx in range(3):
            part = jnp.dot(
                jnp.concatenate(taps[dx], axis=0), second_ref[dx], preferred_element_type=F32
            )
            total = part if total is None else total + part
        rows = GROUP * quarter
        encoded = silu(total).astype(BF16).astype(F32)
        wide = encoded_ref.shape[2]
        for row in range(encoded_ref.shape[0]):
            encoded_ref[row, pl.ds(pl.multiple_of(index * rows, rows), rows), :] = encoded[
                :, row * wide : (row + 1) * wide
            ]
        return carry

    lax.fori_loop(0, hours // GROUP, group, 0)
    copy.wait()
    unroll = 8

    def project(index, total):
        for inner in range(unroll):
            column = index * unroll + inner
            latitudes = range(gain_ref.shape[0])
            rows = jnp.concatenate(
                [encoded_ref[row, pl.ds(column, hours, stride=quarter), :] for row in latitudes],
                axis=1,
            ).astype(BF16)
            gains = jnp.concatenate([gain_ref[row, column] for row in latitudes], axis=0)
            total = total + jnp.dot(rows, gains, preferred_element_type=F32)
        return total

    out_ref[...] = lax.fori_loop(
        0, quarter // unroll, project, jnp.zeros(out_ref.shape, F32)
    )


def encode(fields, conv_in, conv_mid, obs_gain):
    hours, channels, rows, columns = fields.shape
    modes = obs_gain.shape[3]
    first_out = conv_in.shape[0]
    second_out = conv_mid.shape[0]
    depth = channels * rows
    width = (rows // 2) * first_out
    wide = (rows // 4) * second_out
    vmem = pl.BlockSpec(memory_space=pltpu.VMEM)
    return pl.pallas_call(
        encode_kernel,
        out_shape=jax.ShapeDtypeStruct((hours, modes), F32),
        in_specs=[vmem, vmem, vmem, pl.BlockSpec(memory_space=pl.ANY)],
        out_specs=vmem,
        scratch_shapes=[
            pltpu.VMEM(obs_gain.shape, BF16),
            pltpu.VMEM((rows // 4, hours * columns // 4, second_out), F32),
            pltpu.VMEM((3 * columns // 2, columns), BF16),
            pltpu.VMEM((3, (2 * GROUP - 1) * depth, width), BF16),
            pltpu.VMEM((3, width, wide), BF16),
            pltpu.SemaphoreType.DMA,
        ],
        compiler_params=pltpu.CompilerParams(vmem_limit_bytes=48 * 1024 * 1024),
    )(
        fields.reshape(hours * channels * rows, columns),
        conv_in.transpose(2, 3, 1, 0),
        conv_mid.transpose(2, 3, 1, 0),
        obs_gain,
    )


def encode_split(fields, conv_in, conv_mid, obs_gain):
    below_rows = shifted(fields[:, :, -3:, :], "space", 1)
    hidden = conv_stride(
        jnp.concatenate([below_rows[:, :, -1:, :], fields], axis=2), conv_in, "NCHW"
    )
    hidden = jax.nn.silu(hidden).astype(jnp.bfloat16)
    below_hidden = jax.nn.silu(conv_stride(below_rows, conv_in, "NCHW")).astype(jnp.bfloat16)
    encoded = conv_stride(jnp.concatenate([below_hidden, hidden], axis=2), conv_mid, "NHWC")
    encoded = jax.nn.silu(encoded).astype(jnp.bfloat16)
    partial_sum = jnp.einsum("shwc,hwcm->sm", encoded, obs_gain, preferred_element_type=jnp.float32)
    return lax.psum(partial_sum, "space")


def per_device(fields, conv_in, conv_mid, obs_gain, transition, back_gain, retain):
    hour_count = fields.shape[0]
    count = lax.axis_size("tm")
    levels = (count - 1).bit_length()
    hour_levels = (hour_count - 1).bit_length()
    segs, total, powers = local_matrices(transition, back_gain, retain, levels + hour_levels)
    jump = shifted(total, "tm", 1)
    jumps = [jump]
    older = shifted(total, "tm", 2)
    for level in range(1, levels):
        jump = jnp.dot(older, jump, precision=precise)
        jumps.append(jump)
        if level < levels - 1:
            older = shifted(jump, "tm", 1 << level)

    share = hour_count // lax.axis_size("space")
    if lax.axis_size("space") == 1:
        increments = encode(fields, conv_in, conv_mid, obs_gain)
    else:
        increments = encode_split(fields, conv_in, conv_mid, obs_gain)
    filtered, smoothed = chains(
        increments, retain, transition, segs, jnp.stack(jumps), powers, levels, hour_levels
    )
    offset = lax.axis_index("space") * share
    filtered = lax.dynamic_slice_in_dim(filtered, offset, share, 0)
    smoothed = lax.dynamic_slice_in_dim(smoothed, offset, share, 0)
    return (filtered, smoothed)


def solution(mesh):
    placed = (
        P("tm", None, "space", None),
        P(),
        P(),
        P("space", None, None, None),
        P(),
        P(),
        P("tm", None),
    )
    return jax.shard_map(
        per_device,
        mesh=mesh,
        in_specs=placed,
        out_specs=(P(("tm", "space"), None), P(("tm", "space"), None)),
        check_vma=False,
    )
```

```python
import functools

import jax
import jax.numpy as jnp
from jax import lax
from jax.experimental import pallas as pl
from jax.experimental.pallas import tpu as pltpu
from jax.sharding import PartitionSpec as P

F32 = jnp.float32
BF16 = jnp.bfloat16
SEGMENTS = 4
ROWS = 8
GROUP = 4
QUAD = 4
VMEM_BYTES = 56 * 1024 * 1024


def shifted(value, axis, steps):
    count = lax.axis_size(axis)
    leading, last = (max(0, -steps), min(count, count - steps))
    return lax.ppermute(value, axis, [(source, source + steps) for source in range(leading, last)])


def conv_stride(images, kernel, layout_out):
    return lax.conv_general_dilated(
        images,
        kernel,
        (2, 2),
        ((0, 0), (1, 1)),
        dimension_numbers=("NCHW", "OIHW", layout_out),
        preferred_element_type=jnp.float32,
    )


def split_wide(matrix):
    high = matrix.astype(BF16)
    low = (matrix - high.astype(F32)).astype(BF16)
    return jnp.concatenate([high, low], axis=1)


def times(rows, wide):
    count = rows.shape[0]
    size = wide.shape[1] // 2
    high = rows.astype(BF16).astype(F32)
    parts = jnp.concatenate([high, rows - high], axis=0).astype(BF16)
    full = jnp.dot(parts, wide, preferred_element_type=F32)
    return full[:count, :size] + full[count:, :size] + full[:count, size:]


def widened(row):
    return jnp.broadcast_to(row, (ROWS, row.shape[1]))


def solve_back(rows, power_ref, first, steps):
    for k in range(steps):
        stride = 1 << k
        filler = jnp.zeros((stride, rows.shape[1]), F32)
        ahead = jnp.concatenate([rows[stride:], filler], axis=0)
        rows = rows + times(ahead, power_ref[first + k])
    return rows


def silu(value):
    half = 0.5 * value
    return half + half * jnp.tanh(half)


def one_hot(hits):
    return jnp.where(hits, 1.0, 0.0).astype(BF16)


def fill_weights(conv_in_ref, conv_mid_ref, picks_ref, first_ref, second_ref):
    half, columns = picks_ref.shape[0] // 3, picks_ref.shape[1]
    place = lax.broadcasted_iota(jnp.int32, (half, columns), 0)
    column = lax.broadcasted_iota(jnp.int32, (half, columns), 1)
    j = jnp.where(place < half // 2, 2 * place, 2 * place - half + 1)
    for dx in range(3):
        picks_ref[dx * half : (dx + 1) * half, :] = one_hot(column == 2 * j + dx - 1)
    channels, outs = conv_in_ref.shape[2:]
    depth = first_ref.shape[1] // (2 * GROUP - 1)
    rows = depth // channels
    source = lax.broadcasted_iota(jnp.int32, (depth, 3 * channels), 0)
    tap = lax.broadcasted_iota(jnp.int32, (depth, 3 * channels), 1)
    same = (source // rows) == (tap % channels)
    margin = (GROUP - 1) * depth
    first_ref[...] = jnp.zeros(first_ref.shape, BF16)
    for dx in range(3):
        taps = jnp.concatenate([conv_in_ref[dy, dx].astype(F32) for dy in range(3)], axis=0)
        for r in range(rows // 2):
            spread = one_hot(same & (source % rows == 2 * r + tap // channels - 1))
            block = jnp.dot(spread, taps.astype(BF16), preferred_element_type=F32)
            first_ref[dx, margin : margin + depth, r * outs : (r + 1) * outs] = block.astype(BF16)
    inner, outs = conv_mid_ref.shape[2:]
    second_ref[...] = jnp.zeros(second_ref.shape, BF16)
    for dx in range(3):
        for out_row in range(rows // 4):
            for dy in range(3):
                r = 2 * out_row + dy - 1
                if 0 <= r < rows // 2:
                    second_ref[
                        dx, r * inner : (r + 1) * inner, out_row * outs : (out_row + 1) * outs
                    ] = conv_mid_ref[dy, dx]


def encode_groups(field_ref, picks_ref, first_ref, second_ref, encoded_ref, low, high):
    half = picks_ref.shape[0] // 3
    quarter = half // 2
    depth = first_ref.shape[1] // (2 * GROUP - 1)

    def group(index, carry):
        images = field_ref[pl.ds(pl.multiple_of(index * GROUP * depth, GROUP * depth), GROUP * depth), :]
        picked = lax.dot_general(
            picks_ref[...], images, (((1,), (1,)), ((), ())), preferred_element_type=F32
        ).astype(BF16)
        taps = ([], [], [])
        for hour in range(GROUP):
            start = (GROUP - 1 - hour) * depth
            total = None
            for dx in range(3):
                part = jnp.dot(
                    picked[dx * half : (dx + 1) * half],
                    first_ref[dx, start : start + GROUP * depth, :],
                    preferred_element_type=F32,
                )
                total = part if total is None else total + part
            hidden = silu(total)
            odd = hidden[quarter:]
            before = jnp.concatenate(
                [jnp.zeros((1, hidden.shape[1]), F32), odd[: quarter - 1]], axis=0
            )
            taps[0].append(before.astype(BF16))
            taps[1].append(hidden[:quarter].astype(BF16))
            taps[2].append(odd.astype(BF16))
        total = None
        for dx in range(3):
            part = jnp.dot(
                jnp.concatenate(taps[dx], axis=0), second_ref[dx], preferred_element_type=F32
            )
            total = part if total is None else total + part
        rows = GROUP * quarter
        encoded = silu(total).astype(BF16).astype(F32)
        wide = encoded_ref.shape[2]
        for row in range(encoded_ref.shape[0]):
            encoded_ref[row, pl.ds(pl.multiple_of(index * rows, rows), rows), :] = encoded[
                :, row * wide : (row + 1) * wide
            ]
        return carry

    lax.fori_loop(low, high, group, 0)


def project(encoded_ref, gain_ref, hours):
    columns, modes = gain_ref.shape[1], gain_ref.shape[3]
    unroll = 8

    def some(index, total):
        for inner in range(unroll):
            column = index * unroll + inner
            latitudes = range(gain_ref.shape[0])
            rows = jnp.concatenate(
                [encoded_ref[row, pl.ds(column, hours, stride=columns), :] for row in latitudes],
                axis=1,
            ).astype(BF16)
            gains = jnp.concatenate([gain_ref[row, column] for row in latitudes], axis=0)
            total = total + jnp.dot(rows, gains, preferred_element_type=F32)
        return total

    return lax.fori_loop(0, columns // unroll, some, jnp.zeros((hours, modes), F32))


def whole(wide):
    size = wide.shape[1] // 2
    return wide[:, :size].astype(F32) + wide[:, size:].astype(F32)


class Exchange:
    def __init__(self, box, send, recv, place, radix, stride):
        self.box, self.send, self.recv, self.place = box, send, recv, place
        self.radix, self.stride = radix, stride
        self.mine = lax.rem(lax.div(place, stride), radix)

    def copy(self, step, slot):
        block = lax.rem(self.mine + step, self.radix)
        return pltpu.make_async_remote_copy(
            src_ref=self.box.at[slot],
            dst_ref=self.box.at[slot],
            send_sem=self.send.at[step - 1],
            recv_sem=self.recv.at[step - 1],
            device_id={"tm": self.place + (block - self.mine) * self.stride},
            device_id_type=pl.DeviceIdType.MESH,
        )

    def start(self, value):
        self.box[self.mine] = value
        for step in range(1, self.radix):
            self.copy(step, self.mine).start()

    def finish(self):
        for step in range(1, self.radix):
            self.copy(step, self.mine).wait_send()
            self.copy(step, lax.rem(self.mine + self.radix - step, self.radix)).wait_recv()


def main_kernel(count, encoding, *refs):
    if encoding:
        fields_hbm, conv_in_ref, conv_mid_ref, obs_hbm = refs[:4]
    else:
        inc_ref = refs[0]
    refs = refs[4 if encoding else 1 :]
    transition_hbm, gain_hbm, retain_hbm, filtered_ref, smoothed_ref = refs[:5]
    (
        transition_ref,
        gain_ref,
        retain_ref,
        chain,
        seg_ref,
        power_ref,
        pair_box,
        quad_box,
        quad_prefix,
        top_box,
        pair_row,
        quad_row,
        top_row,
        back_out,
        back_box,
        local_sems,
        pair_send,
        pair_recv,
        quad_send,
        quad_recv,
        top_send,
        top_recv,
        row_send,
        row_recv,
        back_send,
        back_recv,
    ) = refs[5:31]
    if encoding:
        field_ref, obs_ref, encoded_ref, picks_ref, first_ref, second_ref = refs[31:]
    hours, size = retain_ref.shape
    span = hours // SEGMENTS
    hour_levels = (hours - 1).bit_length()
    levels = (count - 1).bit_length()
    tops = count // (2 * QUAD)
    place = lax.axis_index("tm")

    def fetch(source, target, index):
        copy = pltpu.make_async_copy(source, target, local_sems.at[index])
        copy.start()
        return copy

    fetched = [
        fetch(transition_hbm, transition_ref, 0),
        fetch(retain_hbm, retain_ref, 1),
        fetch(gain_hbm, gain_ref, 2),
    ]
    if encoding:
        fetched += [fetch(fields_hbm, field_ref, 3), fetch(obs_hbm, obs_ref, 4)]
    top_box[...] = jnp.zeros(top_box.shape, BF16)

    barrier = pltpu.get_barrier_semaphore()

    def greet(step, carry):
        pl.semaphore_signal(
            barrier,
            inc=1,
            device_id={"tm": lax.rem(place + step, count)},
            device_id_type=pl.DeviceIdType.MESH,
        )
        return carry

    lax.fori_loop(1, count, greet, 0)

    fetched[0].wait()
    fetched[1].wait()
    moved = transition_ref[...].T
    wide = split_wide(moved)
    for k in range(SEGMENTS):
        chain[k] = moved * retain_ref[pl.ds(k * span, 1), :]

    def one(step, carry):
        for k in range(SEGMENTS):
            chain[k] = times(chain[k], wide) * retain_ref[pl.ds(k * span + step, 1), :]
        return carry

    lax.fori_loop(1, span, one, 0)
    for k in range(1, SEGMENTS):
        seg_ref[k - 1] = split_wide(chain[k])
    prefix = chain[0]
    for k in range(1, SEGMENTS):
        seg_ref[SEGMENTS - 2 + k] = split_wide(prefix)
        prefix = times(prefix, seg_ref[k - 1])

    pl.semaphore_wait(barrier, count - 1)
    pairs = Exchange(pair_box, pair_send, pair_recv, place, 2, 1)
    pairs.start(split_wide(prefix))
    groups = hours // GROUP
    if encoding:
        fill_weights(conv_in_ref, conv_mid_ref, picks_ref, first_ref, second_ref)
        fetched[3].wait()
        encode_groups(field_ref, picks_ref, first_ref, second_ref, encoded_ref, 0, 1)
    pairs.finish()
    quads = Exchange(quad_box, quad_send, quad_recv, place, QUAD, 2)
    quads.start(split_wide(times(whole(pair_box[0]), pair_box[1])))
    if encoding:
        encode_groups(field_ref, picks_ref, first_ref, second_ref, encoded_ref, 1, groups)
    fetched[2].wait()
    power = gain_ref[...].T
    for k in range(levels + hour_levels):
        power_wide = split_wide(power)
        power_ref[k] = power_wide
        if k < levels + hour_levels - 1:
            power = times(power, power_wide)
    quads.finish()
    prefix = whole(quad_box[0])
    quad_prefix[0] = jnp.zeros(quad_prefix.shape[1:], BF16)
    for k in range(1, QUAD):
        quad_prefix[k] = split_wide(prefix)
        prefix = times(prefix, quad_box[k])
    top = lax.div(place, 2 * QUAD)
    top_box[top] = split_wide(prefix)

    def top_copy(owner, reader):
        return pltpu.make_async_remote_copy(
            src_ref=top_box.at[owner],
            dst_ref=top_box.at[owner],
            send_sem=top_send.at[reader],
            recv_sem=top_recv.at[owner],
            device_id={"tm": place + (reader - top) * 2 * QUAD},
            device_id_type=pl.DeviceIdType.MESH,
        )

    routes = [(owner, reader) for owner in range(1, tops - 1) for reader in range(owner + 1, tops)]
    for owner, reader in routes:

        @pl.when(top == owner)
        def _():
            top_copy(owner, reader).start()

    if encoding:
        fetched[4].wait()
        increments = project(encoded_ref, obs_ref, hours)
    else:
        increments = inc_ref[...]

    gates = retain_ref[...]
    blank = jnp.zeros((ROWS - SEGMENTS, size), F32)

    def of_step(rows, step):
        picked = [rows[k * span + step : k * span + step + 1] for k in range(SEGMENTS)]
        return jnp.concatenate(picked + [blank], axis=0)

    gate_rows = [of_step(gates, step) for step in range(span)]
    inc_rows = [of_step(increments, step) for step in range(span)]
    state = inc_rows[0]
    for step in range(1, span):
        state = times(state, wide) * gate_rows[step] + inc_rows[step]
    starts = [jnp.zeros((1, size), F32)]
    carry = state[0:1]
    for k in range(1, SEGMENTS):
        starts.append(carry)
        carry = times(widened(carry), seg_ref[k - 1])[0:1] + state[k : k + 1]

    pair_rows = Exchange(pair_row, row_send.at[0], row_recv.at[0], place, 2, 1)
    pair_rows.start(carry)
    pair_rows.finish()
    pair_total = times(widened(pair_row[0]), pair_box[1])[0:1] + pair_row[1]
    quad_rows = Exchange(quad_row, row_send.at[1], row_recv.at[1], place, QUAD, 2)
    quad_rows.start(pair_total)
    quad_rows.finish()
    total = quad_row[0]
    quad_enter = jnp.zeros((1, size), F32)
    for k in range(1, QUAD):
        quad_enter = jnp.where(quads.mine == k, total, quad_enter)
        total = times(widened(total), quad_box[k])[0:1] + quad_row[k]
    top_rows = Exchange(top_row, row_send.at[2], row_recv.at[2], place, tops, 2 * QUAD)
    top_rows.start(total)
    for owner, reader in routes:

        @pl.when(top == reader)
        def _():
            top_copy(owner, reader).wait_recv()

    top_rows.finish()
    total = top_row[0]
    entering = jnp.zeros((1, size), F32)
    for k in range(1, tops):
        entering = jnp.where(top == k, total, entering)
        if k < tops - 1:
            total = times(widened(total), top_box[k])[0:1] + top_row[k]
    entering = quad_enter + jnp.where(
        quads.mine == 0, entering, times(widened(entering), quad_prefix[quads.mine])[0:1]
    )
    entering = jnp.where(
        pairs.mine == 0, entering, times(widened(entering), pair_box[0])[0:1] + pair_row[0]
    )

    opened = [entering]
    for k in range(1, SEGMENTS):
        opened.append(
            times(widened(entering), seg_ref[SEGMENTS - 2 + k])[0:1] + starts[k]
        )
    state = jnp.concatenate(opened + [blank], axis=0)
    states = []
    for step in range(span):
        state = times(state, wide) * gate_rows[step] + inc_rows[step]
        states.append(state)
    filtered = jnp.concatenate(
        [states[step][k : k + 1] for k in range(SEGMENTS) for step in range(span)], axis=0
    )
    filtered_ref[...] = filtered
    gain = power_ref[0]
    carried = times(filtered, wide)
    sources = filtered - times(carried, gain)
    final = place == count - 1
    last_row = carried[hours - 1 : hours]
    boundary = jnp.where(final, last_row, jnp.zeros_like(last_row))
    mask = lax.broadcasted_iota(jnp.int32, (hours, 1), 0) == hours - 1

    def with_end(row):
        return sources + jnp.where(mask, times(widened(row), gain)[0:1], 0.0)

    first_pass = solve_back(with_end(boundary), power_ref, 0, hour_levels)
    back_out[0] = first_pass[0:1]

    def back_copy(step):
        return pltpu.make_async_remote_copy(
            src_ref=back_out.at[0],
            dst_ref=back_box.at[step],
            send_sem=back_send.at[step],
            recv_sem=back_recv.at[step],
            device_id={"tm": lax.rem(place + count - 1 - step, count)},
            device_id_type=pl.DeviceIdType.MESH,
        )

    def back_start(step, carry):
        back_copy(step).start()
        return carry

    def back_wait(step, carry):
        back_copy(step).wait()
        return carry

    lax.fori_loop(0, count - 1, back_start, 0)
    lax.fori_loop(0, count - 1, back_wait, 0)
    rows = jnp.concatenate(
        [back_box[step] for step in range(count - 1)] + [jnp.zeros((1, size), F32)], axis=0
    )
    later = lax.broadcasted_iota(jnp.int32, (count, 1), 0) < count - 1 - place
    rows = jnp.where(later, rows, 0.0)
    after = solve_back(rows, power_ref, hour_levels, levels)[0:1]
    smoothed_ref[...] = solve_back(with_end(after + boundary), power_ref, 0, hour_levels)
    for owner, reader in routes:

        @pl.when(top == owner)
        def _():
            top_copy(owner, reader).wait_send()


def run(count, inputs, transition, back_gain, retain):
    hours, size = retain.shape
    tops = count // (2 * QUAD)
    levels = (count - 1).bit_length() + (hours - 1).bit_length()
    vmem = pl.BlockSpec(memory_space=pltpu.VMEM)
    hbm = pl.BlockSpec(memory_space=pl.ANY)
    dma = pltpu.SemaphoreType.DMA

    def matrices(number):
        return pltpu.VMEM((number, size, 2 * size), BF16)

    def rows(number):
        return pltpu.VMEM((number, 1, size), F32)

    most = max(QUAD, tops)
    scratch = [
        pltpu.VMEM((size, size), F32),
        pltpu.VMEM((size, size), F32),
        pltpu.VMEM((hours, size), F32),
        pltpu.VMEM((SEGMENTS, size, size), F32),
        matrices(2 * SEGMENTS - 2),
        matrices(levels),
        matrices(2),
        matrices(QUAD),
        matrices(QUAD),
        matrices(tops),
        rows(2),
        rows(QUAD),
        rows(tops),
        rows(1),
        rows(count),
        dma((5,)),
        dma((1,)),
        dma((1,)),
        dma((QUAD - 1,)),
        dma((QUAD - 1,)),
        dma((tops,)),
        dma((tops,)),
        dma((3, most)),
        dma((3, most)),
        dma((count,)),
        dma((count,)),
    ]
    encoding = len(inputs) > 1
    if encoding:
        fields, conv_in, conv_mid, obs_gain = inputs
        channels, latitudes, columns = fields.shape[1:]
        depth = channels * latitudes
        width = (latitudes // 2) * conv_in.shape[0]
        wide = (latitudes // 4) * conv_mid.shape[0]
        inputs = (
            fields.reshape(hours * depth, columns),
            conv_in.transpose(2, 3, 1, 0),
            conv_mid.transpose(2, 3, 1, 0),
            obs_gain,
        )
        specs = [hbm, vmem, vmem, hbm]
        scratch += [
            pltpu.VMEM((hours * depth, columns), BF16),
            pltpu.VMEM(obs_gain.shape, BF16),
            pltpu.VMEM((latitudes // 4, hours * columns // 4, conv_mid.shape[0]), F32),
            pltpu.VMEM((3 * columns // 2, columns), BF16),
            pltpu.VMEM((3, (2 * GROUP - 1) * depth, width), BF16),
            pltpu.VMEM((3, width, wide), BF16),
        ]
    else:
        specs = [vmem]
    return pl.pallas_call(
        functools.partial(main_kernel, count, encoding),
        out_shape=(
            jax.ShapeDtypeStruct((hours, size), F32),
            jax.ShapeDtypeStruct((hours, size), F32),
        ),
        in_specs=specs + [hbm] * 3,
        out_specs=[vmem] * 2,
        scratch_shapes=scratch,
        compiler_params=pltpu.CompilerParams(
            collective_id=0, has_side_effects=True, vmem_limit_bytes=VMEM_BYTES
        ),
    )(*inputs, transition, back_gain, retain)


def encode_split(fields, conv_in, conv_mid, obs_gain):
    below_rows = shifted(fields[:, :, -3:, :], "space", 1)
    hidden = conv_stride(
        jnp.concatenate([below_rows[:, :, -1:, :], fields], axis=2), conv_in, "NCHW"
    )
    hidden = jax.nn.silu(hidden).astype(jnp.bfloat16)
    below_hidden = jax.nn.silu(conv_stride(below_rows, conv_in, "NCHW")).astype(jnp.bfloat16)
    encoded = conv_stride(jnp.concatenate([below_hidden, hidden], axis=2), conv_mid, "NHWC")
    encoded = jax.nn.silu(encoded).astype(jnp.bfloat16)
    partial_sum = jnp.einsum("shwc,hwcm->sm", encoded, obs_gain, preferred_element_type=jnp.float32)
    return lax.psum(partial_sum, "space")


def per_device(fields, conv_in, conv_mid, obs_gain, transition, back_gain, retain):
    count = lax.axis_size("tm")
    share = fields.shape[0] // lax.axis_size("space")
    if lax.axis_size("space") == 1:
        inputs = (fields, conv_in, conv_mid, obs_gain)
    else:
        inputs = (encode_split(fields, conv_in, conv_mid, obs_gain),)
    filtered, smoothed = run(count, inputs, transition, back_gain, retain)
    if lax.axis_size("space") == 1:
        return (filtered, smoothed)
    offset = lax.axis_index("space") * share
    filtered = lax.dynamic_slice_in_dim(filtered, offset, share, 0)
    smoothed = lax.dynamic_slice_in_dim(smoothed, offset, share, 0)
    return (filtered, smoothed)


def solution(mesh):
    placed = (
        P("tm", None, "space", None),
        P(),
        P(),
        P("space", None, None, None),
        P(),
        P(),
        P("tm", None),
    )
    return jax.shard_map(
        per_device,
        mesh=mesh,
        in_specs=placed,
        out_specs=(P(("tm", "space"), None), P(("tm", "space"), None)),
        check_vma=False,
    )
```

```python
import functools

import jax
import jax.numpy as jnp
from jax import lax
from jax.experimental import pallas as pl
from jax.experimental.pallas import tpu as pltpu
from jax.sharding import PartitionSpec as P

F32 = jnp.float32
BF16 = jnp.bfloat16
SEGMENTS = 4
ROWS = 8
GROUP = 4
QUAD = 4
VMEM_BYTES = 30 * 1024 * 1024


def shifted(value, axis, steps):
    count = lax.axis_size(axis)
    leading, last = (max(0, -steps), min(count, count - steps))
    return lax.ppermute(value, axis, [(source, source + steps) for source in range(leading, last)])


def conv_stride(images, kernel, layout_out):
    return lax.conv_general_dilated(
        images,
        kernel,
        (2, 2),
        ((0, 0), (1, 1)),
        dimension_numbers=("NCHW", "OIHW", layout_out),
        preferred_element_type=jnp.float32,
    )


def split_wide(matrix):
    high = matrix.astype(BF16)
    low = (matrix - high.astype(F32)).astype(BF16)
    return jnp.concatenate([high, low], axis=1)


def times(rows, wide):
    count = rows.shape[0]
    size = wide.shape[1] // 2
    high = rows.astype(BF16).astype(F32)
    if count >= 128:
        low = (rows - high).astype(BF16)
        full = jnp.dot(high.astype(BF16), wide, preferred_element_type=F32)
        rest = jnp.dot(low, wide[:, :size], preferred_element_type=F32)
        return full[:, :size] + (full[:, size:] + rest)
    parts = jnp.concatenate([high, rows - high], axis=0).astype(BF16)
    full = jnp.dot(parts, wide, preferred_element_type=F32)
    return full[:count, :size] + full[count:, :size] + full[:count, size:]


def widened(row):
    return jnp.broadcast_to(row, (ROWS, row.shape[1]))


def solve_back(rows, power_ref, first, steps):
    for k in range(steps):
        stride = 1 << k
        filler = jnp.zeros((stride, rows.shape[1]), F32)
        ahead = jnp.concatenate([rows[stride:], filler], axis=0)
        rows = rows + times(ahead, power_ref[first + k])
    return rows


def silu(value):
    half = 0.5 * value
    return half + half * jnp.tanh(half)


def one_hot(hits):
    return jnp.where(hits, 1.0, 0.0).astype(BF16)


def fill_weights(conv_in_ref, conv_mid_ref, picks_ref, first_ref, second_ref):
    half, columns = picks_ref.shape[0] // 3, picks_ref.shape[1]
    place = lax.broadcasted_iota(jnp.int32, (half, columns), 0)
    column = lax.broadcasted_iota(jnp.int32, (half, columns), 1)
    j = jnp.where(place < half // 2, 2 * place, 2 * place - half + 1)
    for dx in range(3):
        picks_ref[dx * half : (dx + 1) * half, :] = one_hot(column == 2 * j + dx - 1)
    channels, outs = conv_in_ref.shape[2:]
    depth = first_ref.shape[1] // (2 * GROUP - 1)
    rows = depth // channels
    source = lax.broadcasted_iota(jnp.int32, (depth, 3 * channels), 0)
    tap = lax.broadcasted_iota(jnp.int32, (depth, 3 * channels), 1)
    same = (source // rows) == (tap % channels)
    margin = (GROUP - 1) * depth
    first_ref[...] = jnp.zeros(first_ref.shape, BF16)
    for dx in range(3):
        taps = jnp.concatenate([conv_in_ref[dy, dx].astype(F32) for dy in range(3)], axis=0)
        for r in range(rows // 2):
            spread = one_hot(same & (source % rows == 2 * r + tap // channels - 1))
            block = jnp.dot(spread, taps.astype(BF16), preferred_element_type=F32)
            first_ref[dx, margin : margin + depth, r * outs : (r + 1) * outs] = block.astype(BF16)
    inner, outs = conv_mid_ref.shape[2:]
    second_ref[...] = jnp.zeros(second_ref.shape, BF16)
    for dx in range(3):
        for out_row in range(rows // 4):
            for dy in range(3):
                r = 2 * out_row + dy - 1
                if 0 <= r < rows // 2:
                    second_ref[
                        dx, r * inner : (r + 1) * inner, out_row * outs : (out_row + 1) * outs
                    ] = conv_mid_ref[dy, dx]


def encode_groups(field_ref, picks_ref, first_ref, second_ref, encoded_ref, low, high, beside=None):
    half = picks_ref.shape[0] // 3
    quarter = half // 2
    depth = first_ref.shape[1] // (2 * GROUP - 1)

    def group(index, carry):
        if beside is not None:
            beside(index - low)
        images = field_ref[pl.ds(pl.multiple_of(index * GROUP * depth, GROUP * depth), GROUP * depth), :]
        picked = lax.dot_general(
            picks_ref[...], images, (((1,), (1,)), ((), ())), preferred_element_type=F32
        ).astype(BF16)
        taps = ([], [], [])
        for hour in range(GROUP):
            start = (GROUP - 1 - hour) * depth
            total = None
            for dx in range(3):
                part = jnp.dot(
                    picked[dx * half : (dx + 1) * half],
                    first_ref[dx, start : start + GROUP * depth, :],
                    preferred_element_type=F32,
                )
                total = part if total is None else total + part
            hidden = silu(total)
            odd = hidden[quarter:]
            before = jnp.concatenate(
                [jnp.zeros((1, hidden.shape[1]), F32), odd[: quarter - 1]], axis=0
            )
            taps[0].append(before.astype(BF16))
            taps[1].append(hidden[:quarter].astype(BF16))
            taps[2].append(odd.astype(BF16))
        total = None
        for dx in range(3):
            part = jnp.dot(
                jnp.concatenate(taps[dx], axis=0), second_ref[dx], preferred_element_type=F32
            )
            total = part if total is None else total + part
        rows = GROUP * quarter
        encoded = silu(total).astype(BF16).astype(F32)
        wide = encoded_ref.shape[2]
        for row in range(encoded_ref.shape[0]):
            encoded_ref[row, pl.ds(pl.multiple_of(index * rows, rows), rows), :] = encoded[
                :, row * wide : (row + 1) * wide
            ]
        return carry

    lax.fori_loop(low, high, group, 0)


def project(encoded_ref, gain_ref, hours):
    columns, modes = gain_ref.shape[1], gain_ref.shape[3]
    unroll = 8

    def some(index, total):
        for inner in range(unroll):
            column = index * unroll + inner
            latitudes = range(gain_ref.shape[0])
            rows = jnp.concatenate(
                [encoded_ref[row, pl.ds(column, hours, stride=columns), :] for row in latitudes],
                axis=1,
            ).astype(BF16)
            gains = jnp.concatenate([gain_ref[row, column] for row in latitudes], axis=0)
            total = total + jnp.dot(rows, gains, preferred_element_type=F32)
        return total

    return lax.fori_loop(0, columns // unroll, some, jnp.zeros((hours, modes), F32))


def whole(wide):
    size = wide.shape[1] // 2
    return wide[:, :size].astype(F32) + wide[:, size:].astype(F32)


class Exchange:
    def __init__(self, box, send, recv, place, radix, stride):
        self.box, self.send, self.recv, self.place = box, send, recv, place
        self.radix, self.stride = radix, stride
        self.mine = lax.rem(lax.div(place, stride), radix)

    def copy(self, step, slot):
        block = lax.rem(self.mine + step, self.radix)
        return pltpu.make_async_remote_copy(
            src_ref=self.box.at[slot],
            dst_ref=self.box.at[slot],
            send_sem=self.send.at[step - 1],
            recv_sem=self.recv.at[step - 1],
            device_id={"tm": self.place + (block - self.mine) * self.stride},
            device_id_type=pl.DeviceIdType.MESH,
        )

    def start(self, value):
        self.box[self.mine] = value
        for step in range(1, self.radix):
            self.copy(step, self.mine).start()

    def finish(self):
        for step in range(1, self.radix):
            self.copy(step, self.mine).wait_send()
            self.copy(step, lax.rem(self.mine + self.radix - step, self.radix)).wait_recv()


def main_kernel(count, encoding, *refs):
    if encoding:
        fields_hbm, conv_in_ref, conv_mid_ref, obs_hbm = refs[:4]
    else:
        inc_ref = refs[0]
    refs = refs[4 if encoding else 1 :]
    transition_hbm, gain_hbm, retain_hbm, filtered_ref, smoothed_ref = refs[:5]
    (
        transition_ref,
        gain_ref,
        retain_ref,
        chain,
        seg_ref,
        power_ref,
        pair_box,
        quad_box,
        quad_prefix,
        top_box,
        quad_suffix,
        pair_row,
        out_row,
        all_row,
        back_out,
        back_box,
        local_sems,
        pair_send,
        pair_recv,
        quad_send,
        quad_recv,
        top_send,
        top_recv,
        row_send,
        row_recv,
        pair_row_send,
        pair_row_recv,
        back_send,
        back_recv,
    ) = refs[5:34]
    if encoding:
        field_ref, obs_ref, encoded_ref, picks_ref, first_ref, second_ref = refs[34:]
    hours, size = retain_ref.shape
    span = hours // SEGMENTS
    hour_levels = (hours - 1).bit_length()
    levels = (count - 1).bit_length()
    tops = count // (2 * QUAD)
    place = lax.axis_index("tm")

    def fetch(source, target, index):
        copy = pltpu.make_async_copy(source, target, local_sems.at[index])
        copy.start()
        return copy

    fetched = [
        fetch(transition_hbm, transition_ref, 0),
        fetch(retain_hbm, retain_ref, 1),
        fetch(gain_hbm, gain_ref, 2),
    ]
    if encoding:
        fetched += [fetch(fields_hbm, field_ref, 3), fetch(obs_hbm, obs_ref, 4)]
    top_box[...] = jnp.zeros(top_box.shape, BF16)
    all_row[...] = jnp.zeros(all_row.shape, F32)
    back_box[...] = jnp.zeros(back_box.shape, F32)

    barrier = pltpu.get_barrier_semaphore()

    def greet(step, carry):
        pl.semaphore_signal(
            barrier,
            inc=1,
            device_id={"tm": lax.rem(place + step, count)},
            device_id_type=pl.DeviceIdType.MESH,
        )
        return carry

    lax.fori_loop(1, count, greet, 0)

    fetched[0].wait()
    fetched[1].wait()
    moved = transition_ref[...].T
    wide = split_wide(moved)
    for k in range(SEGMENTS):
        chain[k] = moved * retain_ref[pl.ds(k * span, 1), :]

    def one(step, carry):
        for k in range(SEGMENTS):
            chain[k] = times(chain[k], wide) * retain_ref[pl.ds(k * span + step, 1), :]
        return carry

    lax.fori_loop(1, span, one, 0)
    for k in range(1, SEGMENTS):
        seg_ref[k - 1] = split_wide(chain[k])
    suffix = chain[SEGMENTS - 1]
    for k in range(SEGMENTS - 1, 0, -1):
        seg_ref[2 * SEGMENTS - 3 + k] = split_wide(suffix)
        suffix = times(chain[k - 1], seg_ref[2 * SEGMENTS - 3 + k])

    pl.semaphore_wait(barrier, count - 1)
    pairs = Exchange(pair_box, pair_send, pair_recv, place, 2, 1)
    pairs.start(split_wide(suffix))
    prefix = chain[0]
    for k in range(1, SEGMENTS):
        seg_ref[SEGMENTS - 2 + k] = split_wide(prefix)
        if k < SEGMENTS - 1:
            prefix = times(prefix, seg_ref[k - 1])
    groups = hours // GROUP
    if encoding:
        fill_weights(conv_in_ref, conv_mid_ref, picks_ref, first_ref, second_ref)
        fetched[3].wait()
        encode_groups(field_ref, picks_ref, first_ref, second_ref, encoded_ref, 0, 1)
    pairs.finish()
    quads = Exchange(quad_box, quad_send, quad_recv, place, QUAD, 2)
    quads.start(split_wide(times(whole(pair_box[0]), pair_box[1])))
    fetched[2].wait()
    current = chain.at[0]
    current[...] = gain_ref[...].T
    powers = levels + hour_levels

    def raise_power(index):
        power_wide = split_wide(current[...])
        power_ref[index] = power_wide
        current[...] = times(current[...], power_wide)

    done = 0
    if encoding:
        encode_groups(
            field_ref, picks_ref, first_ref, second_ref, encoded_ref, 1, groups, raise_power
        )
        done = groups - 1
    for k in range(done, powers - 1):
        raise_power(k)
    power_ref[powers - 1] = split_wide(current[...])
    quads.finish()
    quad_suffix[QUAD - 1] = jnp.zeros(quad_suffix.shape[1:], BF16)
    quad_suffix[QUAD - 2] = quad_box[QUAD - 1]
    for k in range(QUAD - 2, 0, -1):
        quad_suffix[k - 1] = split_wide(times(whole(quad_box[k]), quad_suffix[k]))
    suffix = times(whole(quad_box[0]), quad_suffix[0])
    top = lax.div(place, 2 * QUAD)
    top_box[top] = split_wide(suffix)

    def top_copy(owner, reader):
        return pltpu.make_async_remote_copy(
            src_ref=top_box.at[owner],
            dst_ref=top_box.at[owner],
            send_sem=top_send.at[reader],
            recv_sem=top_recv.at[owner],
            device_id={"tm": place + (reader - top) * 2 * QUAD},
            device_id_type=pl.DeviceIdType.MESH,
        )

    routes = [(owner, reader) for owner in range(1, tops - 1) for reader in range(owner + 1, tops)]
    for owner, reader in routes:

        @pl.when(top == owner)
        def _():
            top_copy(owner, reader).start()

    quad_prefix[0] = jnp.zeros(quad_prefix.shape[1:], BF16)
    quad_prefix[1] = quad_box[0]
    for k in range(2, QUAD):
        quad_prefix[k] = split_wide(times(whole(quad_prefix[k - 1]), quad_box[k - 1]))
    if encoding:
        fetched[4].wait()
        increments = project(encoded_ref, obs_ref, hours)
    else:
        increments = inc_ref[...]

    gates = retain_ref[...]
    blank = jnp.zeros((ROWS - SEGMENTS, size), F32)

    def of_step(rows, step):
        picked = [rows[k * span + step : k * span + step + 1] for k in range(SEGMENTS)]
        return jnp.concatenate(picked + [blank], axis=0)

    gate_rows = [of_step(gates, step) for step in range(span)]
    inc_rows = [of_step(increments, step) for step in range(span)]
    state = inc_rows[0]
    for step in range(1, span):
        state = times(state, wide) * gate_rows[step] + inc_rows[step]
    carry = state[SEGMENTS - 1 : SEGMENTS]
    for k in range(1, SEGMENTS):
        carry = carry + times(widened(state[k - 1 : k]), seg_ref[2 * SEGMENTS - 3 + k])[0:1]

    pair_rows = Exchange(pair_row, pair_row_send, pair_row_recv, place, 2, 1)
    pair_rows.start(carry)
    to_pair = jnp.where(pairs.mine == 1, carry, times(widened(carry), pair_box[1])[0:1])
    to_plane = jnp.where(
        quads.mine == QUAD - 1, to_pair, times(widened(to_pair), quad_suffix[quads.mine])[0:1]
    )
    plane = 2 * QUAD
    out_row[0] = to_pair
    out_row[1] = to_plane
    all_row[place] = to_pair

    def row_copy(step, peer, slot):
        kind = jnp.where(lax.div(peer, plane) == top, 0, 1)
        return pltpu.make_async_remote_copy(
            src_ref=out_row.at[kind],
            dst_ref=all_row.at[slot],
            send_sem=row_send.at[step],
            recv_sem=row_recv.at[step],
            device_id={"tm": peer},
            device_id_type=pl.DeviceIdType.MESH,
        )

    def row_start(step, carry):
        peer = lax.rem(place + step, count)

        @pl.when(lax.div(peer, plane) >= top)
        def _():
            row_copy(step, peer, place).start()

        return carry

    def row_wait(step, carry):
        peer = lax.rem(place + step, count)
        source = lax.rem(place + count - step, count)

        @pl.when(lax.div(peer, plane) >= top)
        def _():
            row_copy(step, peer, place).wait_send()

        @pl.when(lax.div(source, plane) <= top)
        def _():
            row_copy(step, peer, source).wait_recv()

        return carry

    lax.fori_loop(1, count, row_start, 0)
    starts = [jnp.zeros((1, size), F32)]
    carry = state[0:1]
    for k in range(1, SEGMENTS):
        starts.append(carry)
        if k < SEGMENTS - 1:
            carry = times(widened(carry), seg_ref[k - 1])[0:1] + state[k : k + 1]
    pair_rows.finish()
    lax.fori_loop(1, count, row_wait, 0)
    for owner, reader in routes:

        @pl.when(top == reader)
        def _():
            top_copy(owner, reader).wait_recv()

    base = top * plane
    pair_sums = [all_row[base + 2 * k] + all_row[base + 2 * k + 1] for k in range(QUAD)]
    plane_sums = []
    for k in range(tops - 1):
        total = all_row[k * plane]
        for index in range(1, plane):
            total = total + all_row[k * plane + index]
        plane_sums.append(total)
    total = pair_sums[0]
    quad_enter = jnp.zeros((1, size), F32)
    for k in range(1, QUAD):
        quad_enter = jnp.where(quads.mine == k, total, quad_enter)
        if k < QUAD - 1:
            total = times(widened(total), quad_box[k])[0:1] + pair_sums[k]
    total = plane_sums[0]
    entering = jnp.zeros((1, size), F32)
    for k in range(1, tops):
        entering = jnp.where(top == k, total, entering)
        if k < tops - 1:
            total = times(widened(total), top_box[k])[0:1] + plane_sums[k]
    entering = quad_enter + jnp.where(
        quads.mine == 0, entering, times(widened(entering), quad_prefix[quads.mine])[0:1]
    )
    entering = jnp.where(
        pairs.mine == 0, entering, times(widened(entering), pair_box[0])[0:1] + pair_row[0]
    )

    opened = [entering]
    for k in range(1, SEGMENTS):
        opened.append(
            times(widened(entering), seg_ref[SEGMENTS - 2 + k])[0:1] + starts[k]
        )
    state = jnp.concatenate(opened + [blank], axis=0)
    states = []
    for step in range(span):
        state = times(state, wide) * gate_rows[step] + inc_rows[step]
        states.append(state)
    filtered = jnp.concatenate(
        [states[step][k : k + 1] for k in range(SEGMENTS) for step in range(span)], axis=0
    )
    filtered_ref[...] = filtered
    gain = power_ref[0]
    carried = times(filtered, wide)
    sources = filtered - times(carried, gain)
    final = place == count - 1
    mask = lax.broadcasted_iota(jnp.int32, (hours, 1), 0) == hours - 1
    sources = jnp.where(jnp.logical_and(mask, final), filtered, sources)
    first_pass = solve_back(sources, power_ref, 0, hour_levels)
    back_out[0] = first_pass[0:1]

    def back_copy(step):
        return pltpu.make_async_remote_copy(
            src_ref=back_out.at[0],
            dst_ref=back_box.at[step],
            send_sem=back_send.at[step],
            recv_sem=back_recv.at[step],
            device_id={"tm": place - 1 - step},
            device_id_type=pl.DeviceIdType.MESH,
        )

    def back_start(step, carry):
        @pl.when(step < place)
        def _():
            back_copy(step).start()

        return carry

    def back_wait(step, carry):
        @pl.when(step < place)
        def _():
            back_copy(step).wait_send()

        @pl.when(place + 1 + step < count)
        def _():
            back_copy(step).wait_recv()

        return carry

    lax.fori_loop(0, count - 1, back_start, 0)
    lax.fori_loop(0, count - 1, back_wait, 0)
    rows = jnp.concatenate(
        [back_box[step] for step in range(count - 1)] + [jnp.zeros((1, size), F32)], axis=0
    )
    after = solve_back(rows, power_ref, hour_levels, levels)[0:1]
    ended = sources + jnp.where(mask, times(widened(after), gain)[0:1], 0.0)
    smoothed_ref[...] = solve_back(ended, power_ref, 0, hour_levels)
    for owner, reader in routes:

        @pl.when(top == owner)
        def _():
            top_copy(owner, reader).wait_send()


def run(count, inputs, transition, back_gain, retain):
    hours, size = retain.shape
    tops = count // (2 * QUAD)
    levels = (count - 1).bit_length() + (hours - 1).bit_length()
    vmem = pl.BlockSpec(memory_space=pltpu.VMEM)
    hbm = pl.BlockSpec(memory_space=pl.ANY)
    dma = pltpu.SemaphoreType.DMA

    def matrices(number):
        return pltpu.VMEM((number, size, 2 * size), BF16)

    def rows(number):
        return pltpu.VMEM((number, 1, size), F32)

    scratch = [
        pltpu.VMEM((size, size), F32),
        pltpu.VMEM((size, size), F32),
        pltpu.VMEM((hours, size), F32),
        pltpu.VMEM((SEGMENTS, size, size), F32),
        matrices(3 * SEGMENTS - 3),
        matrices(levels),
        matrices(2),
        matrices(QUAD),
        matrices(QUAD),
        matrices(tops),
        matrices(QUAD),
        rows(2),
        rows(2),
        rows(count),
        rows(1),
        rows(count),
        dma((5,)),
        dma((1,)),
        dma((1,)),
        dma((QUAD - 1,)),
        dma((QUAD - 1,)),
        dma((tops,)),
        dma((tops,)),
        dma((count,)),
        dma((count,)),
        dma((1,)),
        dma((1,)),
        dma((count,)),
        dma((count,)),
    ]
    encoding = len(inputs) > 1
    if encoding:
        fields, conv_in, conv_mid, obs_gain = inputs
        channels, latitudes, columns = fields.shape[1:]
        depth = channels * latitudes
        width = (latitudes // 2) * conv_in.shape[0]
        wide = (latitudes // 4) * conv_mid.shape[0]
        inputs = (
            fields.reshape(hours * depth, columns),
            conv_in.transpose(2, 3, 1, 0),
            conv_mid.transpose(2, 3, 1, 0),
            obs_gain,
        )
        specs = [hbm, vmem, vmem, hbm]
        scratch += [
            pltpu.VMEM((hours * depth, columns), BF16),
            pltpu.VMEM(obs_gain.shape, BF16),
            pltpu.VMEM((latitudes // 4, hours * columns // 4, conv_mid.shape[0]), F32),
            pltpu.VMEM((3 * columns // 2, columns), BF16),
            pltpu.VMEM((3, (2 * GROUP - 1) * depth, width), BF16),
            pltpu.VMEM((3, width, wide), BF16),
        ]
    else:
        specs = [vmem]
    return pl.pallas_call(
        functools.partial(main_kernel, count, encoding),
        out_shape=(
            jax.ShapeDtypeStruct((hours, size), F32),
            jax.ShapeDtypeStruct((hours, size), F32),
        ),
        in_specs=specs + [hbm] * 3,
        out_specs=[vmem] * 2,
        scratch_shapes=scratch,
        compiler_params=pltpu.CompilerParams(
            collective_id=0, has_side_effects=True, vmem_limit_bytes=VMEM_BYTES
        ),
    )(*inputs, transition, back_gain, retain)


def encode_split(fields, conv_in, conv_mid, obs_gain):
    below_rows = shifted(fields[:, :, -3:, :], "space", 1)
    hidden = conv_stride(
        jnp.concatenate([below_rows[:, :, -1:, :], fields], axis=2), conv_in, "NCHW"
    )
    hidden = jax.nn.silu(hidden).astype(jnp.bfloat16)
    below_hidden = jax.nn.silu(conv_stride(below_rows, conv_in, "NCHW")).astype(jnp.bfloat16)
    encoded = conv_stride(jnp.concatenate([below_hidden, hidden], axis=2), conv_mid, "NHWC")
    encoded = jax.nn.silu(encoded).astype(jnp.bfloat16)
    partial_sum = jnp.einsum("shwc,hwcm->sm", encoded, obs_gain, preferred_element_type=jnp.float32)
    return lax.psum(partial_sum, "space")


def per_device(fields, conv_in, conv_mid, obs_gain, transition, back_gain, retain):
    count = lax.axis_size("tm")
    share = fields.shape[0] // lax.axis_size("space")
    if lax.axis_size("space") == 1:
        inputs = (fields, conv_in, conv_mid, obs_gain)
    else:
        inputs = (encode_split(fields, conv_in, conv_mid, obs_gain),)
    filtered, smoothed = run(count, inputs, transition, back_gain, retain)
    if lax.axis_size("space") == 1:
        return (filtered, smoothed)
    offset = lax.axis_index("space") * share
    filtered = lax.dynamic_slice_in_dim(filtered, offset, share, 0)
    smoothed = lax.dynamic_slice_in_dim(smoothed, offset, share, 0)
    return (filtered, smoothed)


def solution(mesh):
    placed = (
        P("tm", None, "space", None),
        P(),
        P(),
        P("space", None, None, None),
        P(),
        P(),
        P("tm", None),
    )
    return jax.shard_map(
        per_device,
        mesh=mesh,
        in_specs=placed,
        out_specs=(P(("tm", "space"), None), P(("tm", "space"), None)),
        check_vma=False,
    )
```

```python
import functools

import jax
import jax.numpy as jnp
from jax import lax
from jax.experimental import pallas as pl
from jax.experimental.pallas import tpu as pltpu
from jax.sharding import PartitionSpec as P

F32 = jnp.float32
BF16 = jnp.bfloat16
SEGMENTS = 8
ROWS = 8
GROUP = 4
QUAD = 4
VMEM_BYTES = 56 * 1024 * 1024


def shifted(value, axis, steps):
    count = lax.axis_size(axis)
    leading, last = (max(0, -steps), min(count, count - steps))
    return lax.ppermute(value, axis, [(source, source + steps) for source in range(leading, last)])


def conv_stride(images, kernel, layout_out):
    return lax.conv_general_dilated(
        images,
        kernel,
        (2, 2),
        ((0, 0), (1, 1)),
        dimension_numbers=("NCHW", "OIHW", layout_out),
        preferred_element_type=jnp.float32,
    )


def split_wide(matrix):
    high = matrix.astype(BF16)
    low = (matrix - high.astype(F32)).astype(BF16)
    return jnp.concatenate([high, low], axis=1)


def times(rows, wide):
    count = rows.shape[0]
    size = wide.shape[1] // 2
    high = rows.astype(BF16).astype(F32)
    if count >= 128:
        low = (rows - high).astype(BF16)
        full = jnp.dot(high.astype(BF16), wide, preferred_element_type=F32)
        rest = jnp.dot(low, wide[:, :size], preferred_element_type=F32)
        return full[:, :size] + (full[:, size:] + rest)
    parts = jnp.concatenate([high, rows - high], axis=0).astype(BF16)
    full = jnp.dot(parts, wide, preferred_element_type=F32)
    return full[:count, :size] + full[count:, :size] + full[:count, size:]


def widened(row):
    return jnp.broadcast_to(row, (ROWS, row.shape[1]))


def solve_back(rows, power_ref, first, steps):
    for k in range(steps):
        stride = 1 << k
        filler = jnp.zeros((stride, rows.shape[1]), F32)
        ahead = jnp.concatenate([rows[stride:], filler], axis=0)
        rows = rows + times(ahead, power_ref[first + k])
    return rows


def silu(value):
    half = 0.5 * value
    return half + half * jnp.tanh(half)


def one_hot(hits):
    return jnp.where(hits, 1.0, 0.0).astype(BF16)


def fill_weights(conv_in_ref, conv_mid_ref, picks_ref, first_ref, second_ref):
    half, columns = picks_ref.shape[0] // 3, picks_ref.shape[1]
    place = lax.broadcasted_iota(jnp.int32, (half, columns), 0)
    column = lax.broadcasted_iota(jnp.int32, (half, columns), 1)
    j = jnp.where(place < half // 2, 2 * place, 2 * place - half + 1)
    for dx in range(3):
        picks_ref[dx * half : (dx + 1) * half, :] = one_hot(column == 2 * j + dx - 1)
    channels, outs = conv_in_ref.shape[2:]
    depth = first_ref.shape[1] // (2 * GROUP - 1)
    rows = depth // channels
    source = lax.broadcasted_iota(jnp.int32, (depth, 3 * channels), 0)
    tap = lax.broadcasted_iota(jnp.int32, (depth, 3 * channels), 1)
    same = (source // rows) == (tap % channels)
    margin = (GROUP - 1) * depth
    first_ref[...] = jnp.zeros(first_ref.shape, BF16)
    for dx in range(3):
        taps = jnp.concatenate([conv_in_ref[dy, dx].astype(F32) for dy in range(3)], axis=0)
        for r in range(rows // 2):
            spread = one_hot(same & (source % rows == 2 * r + tap // channels - 1))
            block = jnp.dot(spread, taps.astype(BF16), preferred_element_type=F32)
            first_ref[dx, margin : margin + depth, r * outs : (r + 1) * outs] = block.astype(BF16)
    inner, outs = conv_mid_ref.shape[2:]
    second_ref[...] = jnp.zeros(second_ref.shape, BF16)
    for dx in range(3):
        for out_row in range(rows // 4):
            for dy in range(3):
                r = 2 * out_row + dy - 1
                if 0 <= r < rows // 2:
                    second_ref[
                        dx, r * inner : (r + 1) * inner, out_row * outs : (out_row + 1) * outs
                    ] = conv_mid_ref[dy, dx]


def encode_groups(field_ref, picks_ref, first_ref, second_ref, encoded_ref, low, high, beside=None):
    half = picks_ref.shape[0] // 3
    quarter = half // 2
    depth = first_ref.shape[1] // (2 * GROUP - 1)

    def group(index, carry):
        if beside is not None:
            beside(index - low)
        images = field_ref[pl.ds(pl.multiple_of(index * GROUP * depth, GROUP * depth), GROUP * depth), :]
        picked = lax.dot_general(
            picks_ref[...], images, (((1,), (1,)), ((), ())), preferred_element_type=F32
        ).astype(BF16)
        taps = ([], [], [])
        for hour in range(GROUP):
            start = (GROUP - 1 - hour) * depth
            total = None
            for dx in range(3):
                part = jnp.dot(
                    picked[dx * half : (dx + 1) * half],
                    first_ref[dx, start : start + GROUP * depth, :],
                    preferred_element_type=F32,
                )
                total = part if total is None else total + part
            hidden = silu(total)
            odd = hidden[quarter:]
            before = jnp.concatenate(
                [jnp.zeros((1, hidden.shape[1]), F32), odd[: quarter - 1]], axis=0
            )
            taps[0].append(before.astype(BF16))
            taps[1].append(hidden[:quarter].astype(BF16))
            taps[2].append(odd.astype(BF16))
        total = None
        for dx in range(3):
            part = jnp.dot(
                jnp.concatenate(taps[dx], axis=0), second_ref[dx], preferred_element_type=F32
            )
            total = part if total is None else total + part
        rows = GROUP * quarter
        encoded = silu(total).astype(BF16).astype(F32)
        wide = encoded_ref.shape[2]
        for row in range(encoded_ref.shape[0]):
            encoded_ref[row, pl.ds(pl.multiple_of(index * rows, rows), rows), :] = encoded[
                :, row * wide : (row + 1) * wide
            ]
        return carry

    lax.fori_loop(low, high, group, 0)


def project(encoded_ref, gain_ref, hours):
    columns, modes = gain_ref.shape[1], gain_ref.shape[3]
    unroll = 8

    def some(index, total):
        for inner in range(unroll):
            column = index * unroll + inner
            latitudes = range(gain_ref.shape[0])
            rows = jnp.concatenate(
                [encoded_ref[row, pl.ds(column, hours, stride=columns), :] for row in latitudes],
                axis=1,
            ).astype(BF16)
            gains = jnp.concatenate([gain_ref[row, column] for row in latitudes], axis=0)
            total = total + jnp.dot(rows, gains, preferred_element_type=F32)
        return total

    return lax.fori_loop(0, columns // unroll, some, jnp.zeros((hours, modes), F32))


def whole(wide):
    size = wide.shape[1] // 2
    return wide[:, :size].astype(F32) + wide[:, size:].astype(F32)


class Exchange:
    def __init__(self, box, send, recv, place, radix, stride, rows=None):
        self.rows = rows
        self.box, self.send, self.recv, self.place = box, send, recv, place
        self.radix, self.stride = radix, stride
        self.mine = lax.rem(lax.div(place, stride), radix)

    def copy(self, step, slot):
        block = lax.rem(self.mine + step, self.radix)
        part = self.box.at[slot] if self.rows is None else self.box.at[slot, self.rows]
        return pltpu.make_async_remote_copy(
            src_ref=part,
            dst_ref=part,
            send_sem=self.send.at[step - 1],
            recv_sem=self.recv.at[step - 1],
            device_id={"tm": self.place + (block - self.mine) * self.stride},
            device_id_type=pl.DeviceIdType.MESH,
        )

    def start(self, value):
        self.box[self.mine] = value
        for step in range(1, self.radix):
            self.copy(step, self.mine).start()

    def finish(self):
        for step in range(1, self.radix):
            self.copy(step, self.mine).wait_send()
            self.copy(step, lax.rem(self.mine + self.radix - step, self.radix)).wait_recv()


def main_kernel(count, encoding, *refs):
    if encoding:
        fields_hbm, conv_in_ref, conv_mid_ref, obs_hbm = refs[:4]
    else:
        inc_ref = refs[0]
    refs = refs[4 if encoding else 1 :]
    transition_hbm, gain_hbm, retain_hbm, filtered_ref, smoothed_ref = refs[:5]
    (
        transition_ref,
        gain_ref,
        retain_ref,
        chain,
        seg_ref,
        power_ref,
        pair_box,
        quad_box,
        quad_prefix,
        top_box,
        quad_suffix,
        pair_row,
        out_row,
        all_row,
        back_out,
        back_box,
        local_sems,
        pair_send,
        pair_recv,
        quad_send,
        quad_recv,
        top_send,
        top_recv,
        row_send,
        row_recv,
        pair_row_send,
        pair_row_recv,
        quad_pass_send,
        quad_pass_recv,
        top_pass_send,
        top_pass_recv,
        back_send,
        back_recv,
    ) = refs[5:38]
    if encoding:
        field_ref, obs_ref, encoded_ref, picks_ref, first_ref, second_ref = refs[38:]
    hours, size = retain_ref.shape
    span = hours // SEGMENTS
    hour_levels = (hours - 1).bit_length()
    levels = (count - 1).bit_length()
    tops = count // (2 * QUAD)
    place = lax.axis_index("tm")

    def fetch(source, target, index):
        copy = pltpu.make_async_copy(source, target, local_sems.at[index])
        copy.start()
        return copy

    fetched = [
        fetch(transition_hbm, transition_ref, 0),
        fetch(retain_hbm, retain_ref, 1),
        fetch(gain_hbm, gain_ref, 2),
    ]
    if encoding:
        fetched += [fetch(fields_hbm, field_ref, 3), fetch(obs_hbm, obs_ref, 4)]
    top_box[...] = jnp.zeros(top_box.shape, BF16)
    all_row[...] = jnp.zeros(all_row.shape, F32)
    back_box[...] = jnp.zeros(back_box.shape, F32)

    barrier = pltpu.get_barrier_semaphore()

    def greet(step, carry):
        pl.semaphore_signal(
            barrier,
            inc=1,
            device_id={"tm": lax.rem(place + step, count)},
            device_id_type=pl.DeviceIdType.MESH,
        )
        return carry

    lax.fori_loop(1, count, greet, 0)

    fetched[0].wait()
    fetched[1].wait()
    moved = transition_ref[...].T
    wide = split_wide(moved)
    for k in range(SEGMENTS):
        chain[k] = moved * retain_ref[pl.ds(k * span, 1), :]

    def one(step, carry):
        for k in range(SEGMENTS):
            chain[k] = times(chain[k], wide) * retain_ref[pl.ds(k * span + step, 1), :]
        return carry

    lax.fori_loop(1, span, one, 0)
    for k in range(1, SEGMENTS):
        seg_ref[k - 1] = split_wide(chain[k])
    suffix = chain[SEGMENTS - 1]
    for k in range(SEGMENTS - 1, 0, -1):
        seg_ref[2 * SEGMENTS - 3 + k] = split_wide(suffix)
        suffix = times(chain[k - 1], seg_ref[2 * SEGMENTS - 3 + k])

    pl.semaphore_wait(barrier, count - 1)
    pairs = Exchange(pair_box, pair_send, pair_recv, place, 2, 1)
    pairs.start(split_wide(suffix))
    prefix = chain[0]
    for k in range(1, SEGMENTS):
        seg_ref[SEGMENTS - 2 + k] = split_wide(prefix)
        if k < SEGMENTS - 1:
            prefix = times(prefix, seg_ref[k - 1])
    groups = hours // GROUP
    if encoding:
        fill_weights(conv_in_ref, conv_mid_ref, picks_ref, first_ref, second_ref)
        fetched[3].wait()
        encode_groups(field_ref, picks_ref, first_ref, second_ref, encoded_ref, 0, 1)
    pairs.finish()
    middle = size // 2
    half = pl.ds(pl.multiple_of(pairs.mine * middle, middle), middle)
    other_half = pl.ds(pl.multiple_of((1 - pairs.mine) * middle, middle), middle)
    partner = place + 1 - 2 * pairs.mine

    def pass_on(box, slot, rows, send, recv):
        return pltpu.make_async_remote_copy(
            src_ref=box.at[slot, rows],
            dst_ref=box.at[slot, rows],
            send_sem=send,
            recv_sem=recv,
            device_id={"tm": partner},
            device_id_type=pl.DeviceIdType.MESH,
        )

    quads = Exchange(quad_box, quad_send, quad_recv, place, QUAD, 2, half)
    quads.start(split_wide(times(whole(pair_box[0]), pair_box[1])))
    fetched[2].wait()
    current = chain.at[0]
    current[...] = gain_ref[...].T
    powers = levels + hour_levels

    def raise_power(index):
        power_wide = split_wide(current[...])
        power_ref[index] = power_wide
        current[...] = times(current[...], power_wide)

    def quad_pass(step, rows):
        slot = lax.rem(quads.mine + QUAD - step, QUAD)
        return pass_on(quad_box, slot, rows, quad_pass_send.at[step - 1], quad_pass_recv.at[step - 1])

    parts = (field_ref, picks_ref, first_ref, second_ref, encoded_ref) if encoding else ()
    early = groups - 2
    done = 0
    if encoding:
        encode_groups(*parts, 1, early, raise_power)
        done = early - 1
    for k in range(done, powers - 1):
        raise_power(k)
    power_ref[powers - 1] = split_wide(current[...])
    quads.finish()
    for step in range(1, QUAD):
        quad_pass(step, half).start()
    if encoding:
        encode_groups(*parts, early, groups)
    for step in range(1, QUAD):
        quad_pass(step, half).wait_send()
        quad_pass(step, other_half).wait_recv()
    quad_suffix[QUAD - 1] = jnp.zeros(quad_suffix.shape[1:], BF16)
    quad_suffix[QUAD - 2] = quad_box[QUAD - 1]
    for k in range(QUAD - 2, 0, -1):
        quad_suffix[k - 1] = split_wide(times(whole(quad_box[k]), quad_suffix[k]))
    suffix = times(whole(quad_box[0]), quad_suffix[0])
    top = lax.div(place, 2 * QUAD)
    top_box[top] = split_wide(suffix)

    def top_copy(owner, reader):
        return pltpu.make_async_remote_copy(
            src_ref=top_box.at[owner, half],
            dst_ref=top_box.at[owner, half],
            send_sem=top_send.at[reader],
            recv_sem=top_recv.at[owner],
            device_id={"tm": place + (reader - top) * 2 * QUAD},
            device_id_type=pl.DeviceIdType.MESH,
        )

    routes = [(owner, reader) for owner in range(1, tops - 1) for reader in range(owner + 1, tops)]
    for owner, reader in routes:

        @pl.when(top == owner)
        def _():
            top_copy(owner, reader).start()

    quad_prefix[0] = jnp.zeros(quad_prefix.shape[1:], BF16)
    quad_prefix[1] = quad_box[0]
    for k in range(2, QUAD):
        quad_prefix[k] = split_wide(times(whole(quad_prefix[k - 1]), quad_box[k - 1]))
    if encoding:
        fetched[4].wait()
        increments = project(encoded_ref, obs_ref, hours)
    else:
        increments = inc_ref[...]

    gates = retain_ref[...]
    blank = [jnp.zeros((ROWS - SEGMENTS, size), F32)] if ROWS > SEGMENTS else []

    def of_step(rows, step):
        picked = [rows[k * span + step : k * span + step + 1] for k in range(SEGMENTS)]
        return jnp.concatenate(picked + blank, axis=0)

    gate_rows = [of_step(gates, step) for step in range(span)]
    inc_rows = [of_step(increments, step) for step in range(span)]
    state = inc_rows[0]
    for step in range(1, span):
        state = times(state, wide) * gate_rows[step] + inc_rows[step]
    carry = state[SEGMENTS - 1 : SEGMENTS]
    for k in range(1, SEGMENTS):
        carry = carry + times(widened(state[k - 1 : k]), seg_ref[2 * SEGMENTS - 3 + k])[0:1]

    def top_pass(owner, rows):
        return pass_on(top_box, owner, rows, top_pass_send.at[owner], top_pass_recv.at[owner])

    pair_rows = Exchange(pair_row, pair_row_send, pair_row_recv, place, 2, 1)
    pair_rows.start(carry)
    to_pair = jnp.where(pairs.mine == 1, carry, times(widened(carry), pair_box[1])[0:1])
    to_plane = jnp.where(
        quads.mine == QUAD - 1, to_pair, times(widened(to_pair), quad_suffix[quads.mine])[0:1]
    )
    plane = 2 * QUAD
    out_row[0] = to_pair
    out_row[1] = to_plane
    all_row[place] = to_pair

    def row_copy(step, peer, slot):
        kind = jnp.where(lax.div(peer, plane) == top, 0, 1)
        return pltpu.make_async_remote_copy(
            src_ref=out_row.at[kind],
            dst_ref=all_row.at[slot],
            send_sem=row_send.at[step],
            recv_sem=row_recv.at[step],
            device_id={"tm": peer},
            device_id_type=pl.DeviceIdType.MESH,
        )

    def row_start(step, carry):
        peer = lax.rem(place + step, count)

        @pl.when(lax.div(peer, plane) >= top)
        def _():
            row_copy(step, peer, place).start()

        return carry

    def row_wait(step, carry):
        peer = lax.rem(place + step, count)
        source = lax.rem(place + count - step, count)

        @pl.when(lax.div(peer, plane) >= top)
        def _():
            row_copy(step, peer, place).wait_send()

        @pl.when(lax.div(source, plane) <= top)
        def _():
            row_copy(step, peer, source).wait_recv()

        return carry

    lax.fori_loop(1, count, row_start, 0)
    for owner, reader in routes:

        @pl.when(top == reader)
        def _():
            top_copy(owner, reader).wait_recv()
            top_pass(owner, half).start()

    starts = [jnp.zeros((1, size), F32)]
    carry = state[0:1]
    for k in range(1, SEGMENTS):
        starts.append(carry)
        if k < SEGMENTS - 1:
            carry = times(widened(carry), seg_ref[k - 1])[0:1] + state[k : k + 1]
    pair_rows.finish()
    lax.fori_loop(1, count, row_wait, 0)
    for owner, reader in routes:

        @pl.when(top == reader)
        def _():
            top_pass(owner, half).wait_send()
            top_pass(owner, other_half).wait_recv()

    base = top * plane
    pair_sums = [all_row[base + 2 * k] + all_row[base + 2 * k + 1] for k in range(QUAD)]
    plane_sums = []
    for k in range(tops - 1):
        total = all_row[k * plane]
        for index in range(1, plane):
            total = total + all_row[k * plane + index]
        plane_sums.append(total)
    total = pair_sums[0]
    quad_enter = jnp.zeros((1, size), F32)
    for k in range(1, QUAD):
        quad_enter = jnp.where(quads.mine == k, total, quad_enter)
        if k < QUAD - 1:
            total = times(widened(total), quad_box[k])[0:1] + pair_sums[k]
    total = plane_sums[0]
    entering = jnp.zeros((1, size), F32)
    for k in range(1, tops):
        entering = jnp.where(top == k, total, entering)
        if k < tops - 1:
            total = times(widened(total), top_box[k])[0:1] + plane_sums[k]
    entering = quad_enter + jnp.where(
        quads.mine == 0, entering, times(widened(entering), quad_prefix[quads.mine])[0:1]
    )
    entering = jnp.where(
        pairs.mine == 0, entering, times(widened(entering), pair_box[0])[0:1] + pair_row[0]
    )

    opened = [entering]
    for k in range(1, SEGMENTS):
        opened.append(
            times(widened(entering), seg_ref[SEGMENTS - 2 + k])[0:1] + starts[k]
        )
    state = jnp.concatenate(opened + blank, axis=0)
    states = []
    for step in range(span):
        state = times(state, wide) * gate_rows[step] + inc_rows[step]
        states.append(state)
    filtered = jnp.concatenate(
        [states[step][k : k + 1] for k in range(SEGMENTS) for step in range(span)], axis=0
    )
    filtered_ref[...] = filtered
    gain = power_ref[0]
    carried = times(filtered, wide)
    sources = filtered - times(carried, gain)
    final = place == count - 1
    mask = lax.broadcasted_iota(jnp.int32, (hours, 1), 0) == hours - 1
    sources = jnp.where(jnp.logical_and(mask, final), filtered, sources)
    first_pass = solve_back(sources, power_ref, 0, hour_levels)
    back_out[0] = first_pass[0:1]

    def back_copy(step):
        return pltpu.make_async_remote_copy(
            src_ref=back_out.at[0],
            dst_ref=back_box.at[step],
            send_sem=back_send.at[step],
            recv_sem=back_recv.at[step],
            device_id={"tm": place - 1 - step},
            device_id_type=pl.DeviceIdType.MESH,
        )

    def back_start(step, carry):
        @pl.when(step < place)
        def _():
            back_copy(step).start()

        return carry

    def back_wait(step, carry):
        @pl.when(step < place)
        def _():
            back_copy(step).wait_send()

        @pl.when(place + 1 + step < count)
        def _():
            back_copy(step).wait_recv()

        return carry

    lax.fori_loop(0, count - 1, back_start, 0)
    lax.fori_loop(0, count - 1, back_wait, 0)
    rows = jnp.concatenate(
        [back_box[step] for step in range(count - 1)] + [jnp.zeros((1, size), F32)], axis=0
    )
    after = solve_back(rows, power_ref, hour_levels, levels)[0:1]
    ended = sources + jnp.where(mask, times(widened(after), gain)[0:1], 0.0)
    smoothed_ref[...] = solve_back(ended, power_ref, 0, hour_levels)
    for owner, reader in routes:

        @pl.when(top == owner)
        def _():
            top_copy(owner, reader).wait_send()


def run(count, inputs, transition, back_gain, retain):
    hours, size = retain.shape
    tops = count // (2 * QUAD)
    levels = (count - 1).bit_length() + (hours - 1).bit_length()
    vmem = pl.BlockSpec(memory_space=pltpu.VMEM)
    hbm = pl.BlockSpec(memory_space=pl.ANY)
    dma = pltpu.SemaphoreType.DMA

    def matrices(number):
        return pltpu.VMEM((number, size, 2 * size), BF16)

    def rows(number):
        return pltpu.VMEM((number, 1, size), F32)

    scratch = [
        pltpu.VMEM((size, size), F32),
        pltpu.VMEM((size, size), F32),
        pltpu.VMEM((hours, size), F32),
        pltpu.VMEM((SEGMENTS, size, size), F32),
        matrices(3 * SEGMENTS - 3),
        matrices(levels),
        matrices(2),
        matrices(QUAD),
        matrices(QUAD),
        matrices(tops),
        matrices(QUAD),
        rows(2),
        rows(2),
        rows(count),
        rows(1),
        rows(count),
        dma((5,)),
        dma((1,)),
        dma((1,)),
        dma((QUAD - 1,)),
        dma((QUAD - 1,)),
        dma((tops,)),
        dma((tops,)),
        dma((count,)),
        dma((count,)),
        dma((1,)),
        dma((1,)),
        dma((QUAD - 1,)),
        dma((QUAD - 1,)),
        dma((tops,)),
        dma((tops,)),
        dma((count,)),
        dma((count,)),
    ]
    encoding = len(inputs) > 1
    if encoding:
        fields, conv_in, conv_mid, obs_gain = inputs
        channels, latitudes, columns = fields.shape[1:]
        depth = channels * latitudes
        width = (latitudes // 2) * conv_in.shape[0]
        wide = (latitudes // 4) * conv_mid.shape[0]
        inputs = (
            fields.reshape(hours * depth, columns),
            conv_in.transpose(2, 3, 1, 0),
            conv_mid.transpose(2, 3, 1, 0),
            obs_gain,
        )
        specs = [hbm, vmem, vmem, hbm]
        scratch += [
            pltpu.VMEM((hours * depth, columns), BF16),
            pltpu.VMEM(obs_gain.shape, BF16),
            pltpu.VMEM((latitudes // 4, hours * columns // 4, conv_mid.shape[0]), F32),
            pltpu.VMEM((3 * columns // 2, columns), BF16),
            pltpu.VMEM((3, (2 * GROUP - 1) * depth, width), BF16),
            pltpu.VMEM((3, width, wide), BF16),
        ]
    else:
        specs = [vmem]
    return pl.pallas_call(
        functools.partial(main_kernel, count, encoding),
        out_shape=(
            jax.ShapeDtypeStruct((hours, size), F32),
            jax.ShapeDtypeStruct((hours, size), F32),
        ),
        in_specs=specs + [hbm] * 3,
        out_specs=[vmem] * 2,
        scratch_shapes=scratch,
        compiler_params=pltpu.CompilerParams(
            collective_id=0, has_side_effects=True, vmem_limit_bytes=VMEM_BYTES
        ),
    )(*inputs, transition, back_gain, retain)


def encode_split(fields, conv_in, conv_mid, obs_gain):
    below_rows = shifted(fields[:, :, -3:, :], "space", 1)
    hidden = conv_stride(
        jnp.concatenate([below_rows[:, :, -1:, :], fields], axis=2), conv_in, "NCHW"
    )
    hidden = jax.nn.silu(hidden).astype(jnp.bfloat16)
    below_hidden = jax.nn.silu(conv_stride(below_rows, conv_in, "NCHW")).astype(jnp.bfloat16)
    encoded = conv_stride(jnp.concatenate([below_hidden, hidden], axis=2), conv_mid, "NHWC")
    encoded = jax.nn.silu(encoded).astype(jnp.bfloat16)
    partial_sum = jnp.einsum("shwc,hwcm->sm", encoded, obs_gain, preferred_element_type=jnp.float32)
    return lax.psum(partial_sum, "space")


def deliver_kernel(first_in, second_in, first_out, second_out, sems):
    copies = [
        pltpu.make_async_copy(first_in, first_out, sems.at[0]),
        pltpu.make_async_copy(second_in, second_out, sems.at[1]),
    ]
    for copy in copies:
        copy.start()
    for copy in copies:
        copy.wait()


def deliver(outputs):
    return pl.pallas_call(
        deliver_kernel,
        out_shape=tuple(jax.ShapeDtypeStruct(o.shape, o.dtype) for o in outputs),
        in_specs=[pl.BlockSpec(memory_space=pl.ANY)] * 2,
        out_specs=[pl.BlockSpec(memory_space=pl.ANY)] * 2,
        scratch_shapes=[pltpu.SemaphoreType.DMA((2,))],
        compiler_params=pltpu.CompilerParams(vmem_limit_bytes=VMEM_BYTES),
    )(*outputs)


def per_device(fields, conv_in, conv_mid, obs_gain, transition, back_gain, retain):
    count = lax.axis_size("tm")
    share = fields.shape[0] // lax.axis_size("space")
    if lax.axis_size("space") == 1:
        inputs = (fields, conv_in, conv_mid, obs_gain)
    else:
        inputs = (encode_split(fields, conv_in, conv_mid, obs_gain),)
    filtered, smoothed = deliver(run(count, inputs, transition, back_gain, retain))
    if lax.axis_size("space") == 1:
        return (filtered, smoothed)
    offset = lax.axis_index("space") * share
    filtered = lax.dynamic_slice_in_dim(filtered, offset, share, 0)
    smoothed = lax.dynamic_slice_in_dim(smoothed, offset, share, 0)
    return (filtered, smoothed)


def solution(mesh):
    placed = (
        P("tm", None, "space", None),
        P(),
        P(),
        P("space", None, None, None),
        P(),
        P(),
        P("tm", None),
    )
    return jax.shard_map(
        per_device,
        mesh=mesh,
        in_specs=placed,
        out_specs=(P(("tm", "space"), None), P(("tm", "space"), None)),
        check_vma=False,
    )
```

```python
import functools

import jax
import jax.numpy as jnp
from jax import lax
from jax.experimental import pallas as pl
from jax.experimental.pallas import tpu as pltpu
from jax.sharding import PartitionSpec as P

F32 = jnp.float32
BF16 = jnp.bfloat16
SEGMENTS = 8
ROWS = 8
GROUP = 4
QUAD = 4
VMEM_BYTES = 56 * 1024 * 1024


def shifted(value, axis, steps):
    count = lax.axis_size(axis)
    leading, last = (max(0, -steps), min(count, count - steps))
    return lax.ppermute(value, axis, [(source, source + steps) for source in range(leading, last)])


def conv_stride(images, kernel, layout_out):
    return lax.conv_general_dilated(
        images,
        kernel,
        (2, 2),
        ((0, 0), (1, 1)),
        dimension_numbers=("NCHW", "OIHW", layout_out),
        preferred_element_type=jnp.float32,
    )


def split_wide(matrix):
    high = matrix.astype(BF16)
    low = (matrix - high.astype(F32)).astype(BF16)
    return jnp.concatenate([high, low], axis=1)


def times(rows, wide):
    count = rows.shape[0]
    size = wide.shape[1] // 2
    high = rows.astype(BF16).astype(F32)
    if count >= 128:
        low = (rows - high).astype(BF16)
        full = jnp.dot(high.astype(BF16), wide, preferred_element_type=F32)
        rest = jnp.dot(low, wide[:, :size], preferred_element_type=F32)
        return full[:, :size] + (full[:, size:] + rest)
    parts = jnp.concatenate([high, rows - high], axis=0).astype(BF16)
    full = jnp.dot(parts, wide, preferred_element_type=F32)
    return full[:count, :size] + full[count:, :size] + full[:count, size:]


def widened(row):
    return jnp.broadcast_to(row, (ROWS, row.shape[1]))


def solve_back(rows, power_ref, first, steps):
    for k in range(steps):
        stride = 1 << k
        filler = jnp.zeros((stride, rows.shape[1]), F32)
        ahead = jnp.concatenate([rows[stride:], filler], axis=0)
        rows = rows + times(ahead, power_ref[first + k])
    return rows


def silu(value):
    half = 0.5 * value
    return half + half * jnp.tanh(half)


def one_hot(hits):
    return jnp.where(hits, 1.0, 0.0).astype(BF16)


def fill_weights(conv_in_ref, conv_mid_ref, picks_ref, first_ref, second_ref):
    half, columns = picks_ref.shape[0] // 3, picks_ref.shape[1]
    place = lax.broadcasted_iota(jnp.int32, (half, columns), 0)
    column = lax.broadcasted_iota(jnp.int32, (half, columns), 1)
    j = jnp.where(place < half // 2, 2 * place, 2 * place - half + 1)
    for dx in range(3):
        picks_ref[dx * half : (dx + 1) * half, :] = one_hot(column == 2 * j + dx - 1)
    channels, outs = conv_in_ref.shape[2:]
    depth = first_ref.shape[1] // (2 * GROUP - 1)
    rows = depth // channels
    source = lax.broadcasted_iota(jnp.int32, (depth, 3 * channels), 0)
    tap = lax.broadcasted_iota(jnp.int32, (depth, 3 * channels), 1)
    same = (source // rows) == (tap % channels)
    margin = (GROUP - 1) * depth
    first_ref[...] = jnp.zeros(first_ref.shape, BF16)
    for dx in range(3):
        taps = jnp.concatenate([conv_in_ref[dy, dx].astype(F32) for dy in range(3)], axis=0)
        for r in range(rows // 2):
            spread = one_hot(same & (source % rows == 2 * r + tap // channels - 1))
            block = jnp.dot(spread, taps.astype(BF16), preferred_element_type=F32)
            first_ref[dx, margin : margin + depth, r * outs : (r + 1) * outs] = block.astype(BF16)
    inner, outs = conv_mid_ref.shape[2:]
    second_ref[...] = jnp.zeros(second_ref.shape, BF16)
    for dx in range(3):
        for out_row in range(rows // 4):
            for dy in range(3):
                r = 2 * out_row + dy - 1
                if 0 <= r < rows // 2:
                    second_ref[
                        dx, r * inner : (r + 1) * inner, out_row * outs : (out_row + 1) * outs
                    ] = conv_mid_ref[dy, dx]


def encode_groups(field_ref, picks_ref, first_ref, second_ref, encoded_ref, low, high, beside=None):
    half = picks_ref.shape[0] // 3
    quarter = half // 2
    depth = first_ref.shape[1] // (2 * GROUP - 1)

    def group(index, carry):
        if beside is not None:
            beside(index - low)
        images = field_ref[pl.ds(pl.multiple_of(index * GROUP * depth, GROUP * depth), GROUP * depth), :]
        picked = lax.dot_general(
            picks_ref[...], images, (((1,), (1,)), ((), ())), preferred_element_type=F32
        ).astype(BF16)
        taps = ([], [], [])
        for hour in range(GROUP):
            start = (GROUP - 1 - hour) * depth
            total = None
            for dx in range(3):
                part = jnp.dot(
                    picked[dx * half : (dx + 1) * half],
                    first_ref[dx, start : start + GROUP * depth, :],
                    preferred_element_type=F32,
                )
                total = part if total is None else total + part
            hidden = silu(total)
            odd = hidden[quarter:]
            before = jnp.concatenate(
                [jnp.zeros((1, hidden.shape[1]), F32), odd[: quarter - 1]], axis=0
            )
            taps[0].append(before.astype(BF16))
            taps[1].append(hidden[:quarter].astype(BF16))
            taps[2].append(odd.astype(BF16))
        total = None
        for dx in range(3):
            part = jnp.dot(
                jnp.concatenate(taps[dx], axis=0), second_ref[dx], preferred_element_type=F32
            )
            total = part if total is None else total + part
        rows = GROUP * quarter
        encoded = silu(total).astype(BF16).astype(F32)
        wide = encoded_ref.shape[2]
        for row in range(encoded_ref.shape[0]):
            encoded_ref[row, pl.ds(pl.multiple_of(index * rows, rows), rows), :] = encoded[
                :, row * wide : (row + 1) * wide
            ]
        return carry

    lax.fori_loop(low, high, group, 0)


def project(encoded_ref, gain_ref, hours):
    columns, modes = gain_ref.shape[1], gain_ref.shape[3]
    unroll = 8

    def some(index, total):
        for inner in range(unroll):
            column = index * unroll + inner
            latitudes = range(gain_ref.shape[0])
            rows = jnp.concatenate(
                [encoded_ref[row, pl.ds(column, hours, stride=columns), :] for row in latitudes],
                axis=1,
            ).astype(BF16)
            gains = jnp.concatenate([gain_ref[row, column] for row in latitudes], axis=0)
            total = total + jnp.dot(rows, gains, preferred_element_type=F32)
        return total

    return lax.fori_loop(0, columns // unroll, some, jnp.zeros((hours, modes), F32))


def whole(wide):
    size = wide.shape[1] // 2
    return wide[:, :size].astype(F32) + wide[:, size:].astype(F32)


class Exchange:
    def __init__(self, box, send, recv, place, radix, stride, rows=None):
        self.rows = rows
        self.box, self.send, self.recv, self.place = box, send, recv, place
        self.radix, self.stride = radix, stride
        self.mine = lax.rem(lax.div(place, stride), radix)

    def copy(self, step, slot):
        block = lax.rem(self.mine + step, self.radix)
        part = self.box.at[slot] if self.rows is None else self.box.at[slot, self.rows]
        return pltpu.make_async_remote_copy(
            src_ref=part,
            dst_ref=part,
            send_sem=self.send.at[step - 1],
            recv_sem=self.recv.at[step - 1],
            device_id={"tm": self.place + (block - self.mine) * self.stride},
            device_id_type=pl.DeviceIdType.MESH,
        )

    def start(self, value):
        self.box[self.mine] = value
        for step in range(1, self.radix):
            self.copy(step, self.mine).start()

    def finish(self):
        for step in range(1, self.radix):
            self.copy(step, self.mine).wait_send()
            self.copy(step, lax.rem(self.mine + self.radix - step, self.radix)).wait_recv()


def main_kernel(count, encoding, *refs):
    if encoding:
        fields_hbm, conv_in_ref, conv_mid_ref, obs_hbm = refs[:4]
    else:
        inc_ref = refs[0]
    refs = refs[4 if encoding else 1 :]
    transition_hbm, gain_hbm, retain_hbm, filtered_ref, smoothed_ref = refs[:5]
    (
        transition_ref,
        gain_ref,
        retain_ref,
        chain,
        seg_ref,
        power_ref,
        pair_box,
        quad_box,
        quad_prefix,
        top_box,
        quad_suffix,
        pair_row,
        out_row,
        all_row,
        back_out,
        back_box,
        local_sems,
        pair_send,
        pair_recv,
        quad_send,
        quad_recv,
        top_send,
        top_recv,
        row_send,
        row_recv,
        pair_row_send,
        pair_row_recv,
        quad_pass_send,
        quad_pass_recv,
        top_pass_send,
        top_pass_recv,
        back_send,
        back_recv,
    ) = refs[5:38]
    if encoding:
        field_ref, obs_ref, encoded_ref, picks_ref, first_ref, second_ref = refs[38:]
    hours, size = retain_ref.shape
    span = hours // SEGMENTS
    hour_levels = (hours - 1).bit_length()
    levels = (count - 1).bit_length()
    tops = count // (2 * QUAD)
    place = lax.axis_index("tm")

    def fetch(source, target, index):
        copy = pltpu.make_async_copy(source, target, local_sems.at[index])
        copy.start()
        return copy

    fetched = [
        fetch(transition_hbm, transition_ref, 0),
        fetch(retain_hbm, retain_ref, 1),
        fetch(gain_hbm, gain_ref, 2),
    ]
    if encoding:
        fetched += [fetch(fields_hbm, field_ref, 3), fetch(obs_hbm, obs_ref, 4)]
    top_box[...] = jnp.zeros(top_box.shape, BF16)
    all_row[...] = jnp.zeros(all_row.shape, F32)
    back_box[...] = jnp.zeros(back_box.shape, F32)

    barrier = pltpu.get_barrier_semaphore()

    def greet(step, carry):
        pl.semaphore_signal(
            barrier,
            inc=1,
            device_id={"tm": lax.rem(place + step, count)},
            device_id_type=pl.DeviceIdType.MESH,
        )
        return carry

    lax.fori_loop(1, count, greet, 0)

    fetched[0].wait()
    fetched[1].wait()
    moved = transition_ref[...].T
    wide = split_wide(moved)
    for k in range(SEGMENTS):
        chain[k] = moved * retain_ref[pl.ds(k * span, 1), :]

    def one(step, carry):
        for k in range(SEGMENTS):
            chain[k] = times(chain[k], wide) * retain_ref[pl.ds(k * span + step, 1), :]
        return carry

    lax.fori_loop(1, span, one, 0)
    for k in range(1, SEGMENTS):
        seg_ref[k - 1] = split_wide(chain[k])
    suffix = chain[SEGMENTS - 1]
    for k in range(SEGMENTS - 1, 0, -1):
        seg_ref[2 * SEGMENTS - 3 + k] = split_wide(suffix)
        suffix = times(chain[k - 1], seg_ref[2 * SEGMENTS - 3 + k])

    pl.semaphore_wait(barrier, count - 1)
    pairs = Exchange(pair_box, pair_send, pair_recv, place, 2, 1)
    pairs.start(split_wide(suffix))
    prefix = chain[0]
    for k in range(1, SEGMENTS):
        seg_ref[SEGMENTS - 2 + k] = split_wide(prefix)
        if k < SEGMENTS - 1:
            prefix = times(prefix, seg_ref[k - 1])
    groups = hours // GROUP
    if encoding:
        fill_weights(conv_in_ref, conv_mid_ref, picks_ref, first_ref, second_ref)
        fetched[3].wait()
        encode_groups(field_ref, picks_ref, first_ref, second_ref, encoded_ref, 0, 1)
    pairs.finish()
    middle = size // 2
    half = pl.ds(pl.multiple_of(pairs.mine * middle, middle), middle)
    other_half = pl.ds(pl.multiple_of((1 - pairs.mine) * middle, middle), middle)
    partner = place + 1 - 2 * pairs.mine

    def pass_on(box, slot, rows, send, recv):
        return pltpu.make_async_remote_copy(
            src_ref=box.at[slot, rows],
            dst_ref=box.at[slot, rows],
            send_sem=send,
            recv_sem=recv,
            device_id={"tm": partner},
            device_id_type=pl.DeviceIdType.MESH,
        )

    quads = Exchange(quad_box, quad_send, quad_recv, place, QUAD, 2, half)
    quads.start(split_wide(times(whole(pair_box[0]), pair_box[1])))
    fetched[2].wait()
    current = chain.at[0]
    current[...] = gain_ref[...].T
    powers = levels + hour_levels

    def raise_power(index):
        power_wide = split_wide(current[...])
        power_ref[index] = power_wide
        current[...] = times(current[...], power_wide)

    def quad_pass(step, rows):
        slot = lax.rem(quads.mine + QUAD - step, QUAD)
        return pass_on(quad_box, slot, rows, quad_pass_send.at[step - 1], quad_pass_recv.at[step - 1])

    parts = (field_ref, picks_ref, first_ref, second_ref, encoded_ref) if encoding else ()
    early = groups - 2
    done = 0
    if encoding:
        encode_groups(*parts, 1, early, raise_power)
        done = early - 1
    for k in range(done, powers - 1):
        raise_power(k)
    power_ref[powers - 1] = split_wide(current[...])
    quads.finish()
    for step in range(1, QUAD):
        quad_pass(step, half).start()
    if encoding:
        encode_groups(*parts, early, groups)
    for step in range(1, QUAD):
        quad_pass(step, half).wait_send()
        quad_pass(step, other_half).wait_recv()
    quad_suffix[QUAD - 1] = jnp.zeros(quad_suffix.shape[1:], BF16)
    quad_suffix[QUAD - 2] = quad_box[QUAD - 1]
    for k in range(QUAD - 2, 0, -1):
        quad_suffix[k - 1] = split_wide(times(whole(quad_box[k]), quad_suffix[k]))
    suffix = times(whole(quad_box[0]), quad_suffix[0])
    top = lax.div(place, 2 * QUAD)
    top_box[top] = split_wide(suffix)

    def top_copy(owner, reader):
        return pltpu.make_async_remote_copy(
            src_ref=top_box.at[owner, half],
            dst_ref=top_box.at[owner, half],
            send_sem=top_send.at[reader],
            recv_sem=top_recv.at[owner],
            device_id={"tm": place + (reader - top) * 2 * QUAD},
            device_id_type=pl.DeviceIdType.MESH,
        )

    routes = [(owner, reader) for owner in range(1, tops - 1) for reader in range(owner + 1, tops)]
    for owner, reader in routes:

        @pl.when(top == owner)
        def _():
            top_copy(owner, reader).start()

    quad_prefix[0] = jnp.zeros(quad_prefix.shape[1:], BF16)
    quad_prefix[1] = quad_box[0]
    for k in range(2, QUAD):
        quad_prefix[k] = split_wide(times(whole(quad_prefix[k - 1]), quad_box[k - 1]))
    if encoding:
        fetched[4].wait()
        increments = project(encoded_ref, obs_ref, hours)
    else:
        increments = inc_ref[...]

    gates = retain_ref[...]
    blank = [jnp.zeros((ROWS - SEGMENTS, size), F32)] if ROWS > SEGMENTS else []

    def of_step(rows, step):
        picked = [rows[k * span + step : k * span + step + 1] for k in range(SEGMENTS)]
        return jnp.concatenate(picked + blank, axis=0)

    gate_rows = [of_step(gates, step) for step in range(span)]
    inc_rows = [of_step(increments, step) for step in range(span)]
    state = inc_rows[0]
    for step in range(1, span):
        state = times(state, wide) * gate_rows[step] + inc_rows[step]
    carry = state[SEGMENTS - 1 : SEGMENTS]
    for k in range(1, SEGMENTS):
        carry = carry + times(widened(state[k - 1 : k]), seg_ref[2 * SEGMENTS - 3 + k])[0:1]

    def top_pass(owner, rows):
        return pass_on(top_box, owner, rows, top_pass_send.at[owner], top_pass_recv.at[owner])

    pair_rows = Exchange(pair_row, pair_row_send, pair_row_recv, place, 2, 1)
    pair_rows.start(carry)
    to_pair = jnp.where(pairs.mine == 1, carry, times(widened(carry), pair_box[1])[0:1])
    to_plane = jnp.where(
        quads.mine == QUAD - 1, to_pair, times(widened(to_pair), quad_suffix[quads.mine])[0:1]
    )
    plane = 2 * QUAD
    out_row[0] = to_pair
    out_row[1] = to_plane
    all_row[place] = to_pair

    def row_copy(step, peer, slot):
        kind = jnp.where(lax.div(peer, plane) == top, 0, 1)
        return pltpu.make_async_remote_copy(
            src_ref=out_row.at[kind],
            dst_ref=all_row.at[slot],
            send_sem=row_send.at[step],
            recv_sem=row_recv.at[step],
            device_id={"tm": peer},
            device_id_type=pl.DeviceIdType.MESH,
        )

    def row_start(step, carry):
        peer = lax.rem(place + step, count)

        @pl.when(lax.div(peer, plane) >= top)
        def _():
            row_copy(step, peer, place).start()

        return carry

    def row_wait(step, carry):
        peer = lax.rem(place + step, count)
        source = lax.rem(place + count - step, count)

        @pl.when(lax.div(peer, plane) >= top)
        def _():
            row_copy(step, peer, place).wait_send()

        @pl.when(lax.div(source, plane) <= top)
        def _():
            row_copy(step, peer, source).wait_recv()

        return carry

    lax.fori_loop(1, count, row_start, 0)
    for owner, reader in routes:

        @pl.when(top == reader)
        def _():
            top_copy(owner, reader).wait_recv()
            top_pass(owner, half).start()

    starts = [jnp.zeros((1, size), F32)]
    carry = state[0:1]
    for k in range(1, SEGMENTS):
        starts.append(carry)
        if k < SEGMENTS - 1:
            carry = times(widened(carry), seg_ref[k - 1])[0:1] + state[k : k + 1]
    pair_rows.finish()
    lax.fori_loop(1, count, row_wait, 0)
    for owner, reader in routes:

        @pl.when(top == reader)
        def _():
            top_pass(owner, half).wait_send()
            top_pass(owner, other_half).wait_recv()

    base = top * plane
    pair_sums = [all_row[base + 2 * k] + all_row[base + 2 * k + 1] for k in range(QUAD)]
    plane_sums = []
    for k in range(tops - 1):
        total = all_row[k * plane]
        for index in range(1, plane):
            total = total + all_row[k * plane + index]
        plane_sums.append(total)
    total = pair_sums[0]
    quad_enter = jnp.zeros((1, size), F32)
    for k in range(1, QUAD):
        quad_enter = jnp.where(quads.mine == k, total, quad_enter)
        if k < QUAD - 1:
            total = times(widened(total), quad_box[k])[0:1] + pair_sums[k]
    total = plane_sums[0]
    entering = jnp.zeros((1, size), F32)
    for k in range(1, tops):
        entering = jnp.where(top == k, total, entering)
        if k < tops - 1:
            total = times(widened(total), top_box[k])[0:1] + plane_sums[k]
    entering = quad_enter + jnp.where(
        quads.mine == 0, entering, times(widened(entering), quad_prefix[quads.mine])[0:1]
    )
    entering = jnp.where(
        pairs.mine == 0, entering, times(widened(entering), pair_box[0])[0:1] + pair_row[0]
    )

    opened = [entering]
    for k in range(1, SEGMENTS):
        opened.append(
            times(widened(entering), seg_ref[SEGMENTS - 2 + k])[0:1] + starts[k]
        )
    state = jnp.concatenate(opened + blank, axis=0)
    states = []
    for step in range(span):
        state = times(state, wide) * gate_rows[step] + inc_rows[step]
        states.append(state)
    filtered = jnp.concatenate(
        [states[step][k : k + 1] for k in range(SEGMENTS) for step in range(span)], axis=0
    )
    filtered_ref[...] = filtered
    gain = power_ref[0]
    carried = times(filtered, wide)
    sources = filtered - times(carried, gain)
    final = place == count - 1
    mask = lax.broadcasted_iota(jnp.int32, (hours, 1), 0) == hours - 1
    sources = jnp.where(jnp.logical_and(mask, final), filtered, sources)
    first_pass = solve_back(sources, power_ref, 0, hour_levels)
    back_out[0] = first_pass[0:1]

    def back_copy(step):
        return pltpu.make_async_remote_copy(
            src_ref=back_out.at[0],
            dst_ref=back_box.at[step],
            send_sem=back_send.at[step],
            recv_sem=back_recv.at[step],
            device_id={"tm": place - 1 - step},
            device_id_type=pl.DeviceIdType.MESH,
        )

    def back_start(step, carry):
        @pl.when(step < place)
        def _():
            back_copy(step).start()

        return carry

    def back_wait(step, carry):
        @pl.when(step < place)
        def _():
            back_copy(step).wait_send()

        @pl.when(place + 1 + step < count)
        def _():
            back_copy(step).wait_recv()

        return carry

    lax.fori_loop(0, count - 1, back_start, 0)
    lax.fori_loop(0, count - 1, back_wait, 0)
    rows = jnp.concatenate(
        [back_box[step] for step in range(count - 1)] + [jnp.zeros((1, size), F32)], axis=0
    )
    after = solve_back(rows, power_ref, hour_levels, levels)[0:1]
    ended = sources + jnp.where(mask, times(widened(after), gain)[0:1], 0.0)
    smoothed_ref[...] = solve_back(ended, power_ref, 0, hour_levels)
    for owner, reader in routes:

        @pl.when(top == owner)
        def _():
            top_copy(owner, reader).wait_send()


def run(count, inputs, transition, back_gain, retain):
    hours, size = retain.shape
    tops = count // (2 * QUAD)
    levels = (count - 1).bit_length() + (hours - 1).bit_length()
    vmem = pl.BlockSpec(memory_space=pltpu.VMEM)
    hbm = pl.BlockSpec(memory_space=pl.ANY)
    dma = pltpu.SemaphoreType.DMA

    def matrices(number):
        return pltpu.VMEM((number, size, 2 * size), BF16)

    def rows(number):
        return pltpu.VMEM((number, 1, size), F32)

    scratch = [
        pltpu.VMEM((size, size), F32),
        pltpu.VMEM((size, size), F32),
        pltpu.VMEM((hours, size), F32),
        pltpu.VMEM((SEGMENTS, size, size), F32),
        matrices(3 * SEGMENTS - 3),
        matrices(levels),
        matrices(2),
        matrices(QUAD),
        matrices(QUAD),
        matrices(tops),
        matrices(QUAD),
        rows(2),
        rows(2),
        rows(count),
        rows(1),
        rows(count),
        dma((5,)),
        dma((1,)),
        dma((1,)),
        dma((QUAD - 1,)),
        dma((QUAD - 1,)),
        dma((tops,)),
        dma((tops,)),
        dma((count,)),
        dma((count,)),
        dma((1,)),
        dma((1,)),
        dma((QUAD - 1,)),
        dma((QUAD - 1,)),
        dma((tops,)),
        dma((tops,)),
        dma((count,)),
        dma((count,)),
    ]
    encoding = len(inputs) > 1
    if encoding:
        fields, conv_in, conv_mid, obs_gain = inputs
        channels, latitudes, columns = fields.shape[1:]
        depth = channels * latitudes
        width = (latitudes // 2) * conv_in.shape[0]
        wide = (latitudes // 4) * conv_mid.shape[0]
        inputs = (
            fields.reshape(hours * depth, columns),
            conv_in.transpose(2, 3, 1, 0),
            conv_mid.transpose(2, 3, 1, 0),
            obs_gain,
        )
        specs = [hbm, vmem, vmem, hbm]
        scratch += [
            pltpu.VMEM((hours * depth, columns), BF16),
            pltpu.VMEM(obs_gain.shape, BF16),
            pltpu.VMEM((latitudes // 4, hours * columns // 4, conv_mid.shape[0]), F32),
            pltpu.VMEM((3 * columns // 2, columns), BF16),
            pltpu.VMEM((3, (2 * GROUP - 1) * depth, width), BF16),
            pltpu.VMEM((3, width, wide), BF16),
        ]
    else:
        specs = [vmem]
    return pl.pallas_call(
        functools.partial(main_kernel, count, encoding),
        out_shape=(
            jax.ShapeDtypeStruct((hours, size), F32),
            jax.ShapeDtypeStruct((hours, size), F32),
        ),
        in_specs=specs + [hbm] * 3,
        out_specs=[vmem] * 2,
        scratch_shapes=scratch,
        compiler_params=pltpu.CompilerParams(
            collective_id=0, has_side_effects=True, vmem_limit_bytes=VMEM_BYTES
        ),
    )(*inputs, transition, back_gain, retain)


def encode_split(fields, conv_in, conv_mid, obs_gain):
    below_rows = shifted(fields[:, :, -3:, :], "space", 1)
    hidden = conv_stride(
        jnp.concatenate([below_rows[:, :, -1:, :], fields], axis=2), conv_in, "NCHW"
    )
    hidden = jax.nn.silu(hidden).astype(jnp.bfloat16)
    below_hidden = jax.nn.silu(conv_stride(below_rows, conv_in, "NCHW")).astype(jnp.bfloat16)
    encoded = conv_stride(jnp.concatenate([below_hidden, hidden], axis=2), conv_mid, "NHWC")
    encoded = jax.nn.silu(encoded).astype(jnp.bfloat16)
    partial_sum = jnp.einsum("shwc,hwcm->sm", encoded, obs_gain, preferred_element_type=jnp.float32)
    return lax.psum(partial_sum, "space")


def deliver_kernel(first_in, second_in, first_out, second_out):
    first_out[...] = first_in[...]
    second_out[...] = second_in[...]


def deliver(outputs):
    return pl.pallas_call(
        deliver_kernel,
        out_shape=tuple(jax.ShapeDtypeStruct(o.shape, o.dtype) for o in outputs),
        in_specs=[pl.BlockSpec(memory_space=pltpu.VMEM)] * 2,
        out_specs=[pl.BlockSpec(memory_space=pltpu.VMEM)] * 2,
        compiler_params=pltpu.CompilerParams(vmem_limit_bytes=VMEM_BYTES),
    )(*outputs)


def per_device(fields, conv_in, conv_mid, obs_gain, transition, back_gain, retain):
    count = lax.axis_size("tm")
    share = fields.shape[0] // lax.axis_size("space")
    if lax.axis_size("space") == 1:
        inputs = (fields, conv_in, conv_mid, obs_gain)
    else:
        inputs = (encode_split(fields, conv_in, conv_mid, obs_gain),)
    filtered, smoothed = deliver(run(count, inputs, transition, back_gain, retain))
    if lax.axis_size("space") == 1:
        return (filtered, smoothed)
    offset = lax.axis_index("space") * share
    filtered = lax.dynamic_slice_in_dim(filtered, offset, share, 0)
    smoothed = lax.dynamic_slice_in_dim(smoothed, offset, share, 0)
    return (filtered, smoothed)


def solution(mesh):
    placed = (
        P("tm", None, "space", None),
        P(),
        P(),
        P("space", None, None, None),
        P(),
        P(),
        P("tm", None),
    )
    return jax.shard_map(
        per_device,
        mesh=mesh,
        in_specs=placed,
        out_specs=(P(("tm", "space"), None), P(("tm", "space"), None)),
        check_vma=False,
    )
```
